32 devices in a mesh: row: 4 (over y, core), col: 8 (over z, x).
Axes of the slice: x: 2, y: 2, z: 4, core: 2. Of those that a mesh axis runs over, the one named last changes fastest.
Arguments:
- features: bfloat16 [16384, 256], P(('row', 'col')), may hold values from -6 to 6
- tile_values: bfloat16 [64, 64, 256, 256], P('col', 'row'), may hold values from 0 to 1, as said below
- tile_cols: int32 [64, 64], P('col', 'row'), may hold values from 0 to 15
- tile_counts: int32 [64, 4], P('col', 'row'), may hold values from 1 to 16, as said below
- weight: bfloat16 [256, 256], replicated, may hold values from -0.375 to 0.375
- bias: float32 [256], replicated, may hold values from -3 to 3
- cotangent: bfloat16 [16384, 256], P(('col', 'row')), may hold values from -6 to 6
Outputs:
- layer_out: bfloat16 [16384, 256], P(('col', 'row'))
- feature_grad: bfloat16 [16384, 256], P(('row', 'col'))
- weight_grad: float32 [256, 256], replicated
- bias_grad: float32 [256], replicated
The draws below stay inside these ranges and needn't reach their ends.
Inputs may be any that keep to these rules, and one draw needn't show every extreme that they name: `tile_values`: nonnegative edge weights. `tile_counts`: every draw has some entry equal to 16; the loads differ between the devices' blocks.
All inputs are finite; a program needn't handle non-finite values.
Results may differ from the reference program's by a relative error of at most 0.025.
Values may be sent and summed in bfloat16 or wider, within the bound.
No kernel may reach another device: no remote copies, remote signals or barrier semaphores. Data moves between devices by JAX's collectives and lax.ppermute only.
A program may use at most 128 MiB of HBM per device.

```python
import math
import jax
import jax.numpy as jnp
from jax import lax

HID = 256
TILE = 256
SLOTS = 16
NODES = 16384
ROW_TILES = 8
COL_TILES = 16
N_ROW = 4
N_COL = 8


def draw_tile_values(key, part):
    shape = (N_COL * ROW_TILES, N_ROW * SLOTS, TILE, TILE)
    spread = (3.0 / (N_ROW * SLOTS * TILE)) ** 0.5
    values = jax.random.uniform(key, shape, jnp.float32, 0.0, 1.0) * spread
    return values.astype(jnp.bfloat16)


def draw_tile_counts(key, part):
    level_key = jax.random.fold_in(key, 11)
    count_key = jax.random.fold_in(key, 12)
    place_key = jax.random.fold_in(key, 13)
    levels = jax.random.randint(level_key, (N_COL, N_ROW), 0, 4)
    limits = jnp.maximum(1, SLOTS // 2 ** levels)
    limits = jnp.repeat(limits, ROW_TILES, axis=0)
    counts = jax.random.randint(count_key, (N_COL * ROW_TILES, N_ROW), 1, limits + 1)
    chosen = jax.random.randint(place_key, (), 0, N_COL * ROW_TILES * N_ROW)
    flat_iota = jnp.arange(N_COL * ROW_TILES * N_ROW, dtype=jnp.int32).reshape(N_COL * ROW_TILES, N_ROW)
    counts = jnp.where(flat_iota == chosen, SLOTS, counts)
    return counts.astype(jnp.int32)


def with_ends(values, rng, smallest, high):
    index_at = [jax.random.randint(jax.random.fold_in(rng, axis), (), 0, length) for axis, length in enumerate(values.shape)]
    longest = values.shape.index(max(values.shape))
    next_to = index_at[:longest] + [(index_at[longest] + 1) % values.shape[longest]] + index_at[longest + 1:]
    return values.at[tuple(index_at)].set(smallest).at[tuple(next_to)].set(high)


def block_scale(key, shape, cuts, low, high):
    level, own = 1.0, jax.random.fold_in(key, 6)
    for dim, shards_of in cuts:
        steps = jnp.exp(jax.random.uniform(jax.random.fold_in(own, dim), (shards_of,), jnp.float32, low / len(cuts), high / len(cuts)))
        level = level * jnp.repeat(steps, shape[dim] // shards_of).reshape([-1 if axis == dim else 1 for axis in range(len(shape))])
    return level


def scatter_about(own_key, extent, width, limit, pieces=(), kind=jnp.bfloat16):
    array = jax.random.normal(own_key, extent, jnp.float32) * width
    if len(pieces) > 0:
        array = block_scale(own_key, extent, pieces, -0.22, 0.18) * array
    return jnp.clip(array, min=-limit, max=limit).astype(kind)


def setup_inputs(seed: int = 0) -> dict:
    streams_of = jax.random.split(jax.random.key(seed), 8)
    return {
        "features": scatter_about(streams_of[0], (NODES, HID), 1.0, 6.0, ((0, 32),)),
        "tile_values": draw_tile_values(jax.random.fold_in(streams_of[7], 71), 0),
        "tile_cols": with_ends(jax.random.randint(streams_of[2], (N_COL * ROW_TILES, N_ROW * SLOTS), 0, COL_TILES), jax.random.fold_in(streams_of[2], 1), 0, COL_TILES - 1).astype(jnp.int32),
        "tile_counts": draw_tile_counts(jax.random.fold_in(streams_of[7], 71), 0),
        "weight": scatter_about(streams_of[4], (HID, HID), HID ** -0.5, 0.375),
        "bias": scatter_about(streams_of[5], (HID,), 0.5, 3.0, (), jnp.float32),
        "cotangent": scatter_about(streams_of[6], (NODES, HID), 1.0, 6.0, ((0, 32),)),
    }


def reference(features, tile_values, tile_cols, tile_counts, weight, bias, cotangent):
    node_total = features.shape[0]
    x_tiles = features.reshape(node_total // TILE, TILE, HID)
    slot_iota = jnp.arange(N_ROW * SLOTS, dtype=jnp.int32)
    source_block = (slot_iota // SLOTS).astype(jnp.int32)
    within_block = (slot_iota % SLOTS).astype(jnp.int32)

    def tile_meta(tile_index):
        source_index = (source_block * COL_TILES + tile_cols[tile_index]).astype(jnp.int32)
        active = (within_block < tile_counts[tile_index][source_block]).astype(jnp.float32)
        return (source_index, active)

    def forward_tile(tile_index):
        source_index, active = tile_meta(tile_index)
        picked = x_tiles[source_index].astype(jnp.float32) * active[:, None, None]
        return jnp.einsum('kij,kjf->if', tile_values[tile_index].astype(jnp.float32), picked)
    tile_range = jnp.arange(N_COL * ROW_TILES, dtype=jnp.int32)
    hidden = lax.map(forward_tile, tile_range).reshape(node_total, HID).astype(jnp.bfloat16)
    preact = jnp.dot(hidden, weight, preferred_element_type=jnp.float32) + bias
    layer_out = jax.nn.silu(preact).astype(jnp.bfloat16)
    sigmoid_value = jax.nn.sigmoid(preact)
    slope = sigmoid_value * (1.0 + preact * (1.0 - sigmoid_value))
    preact_grad = (cotangent.astype(jnp.float32) * slope).astype(jnp.bfloat16)
    grad_scale = 1.0 / math.sqrt(node_total)
    weight_grad = lax.dot_general(hidden, preact_grad, (((0,), (0,)), ((), ())), preferred_element_type=jnp.float32) * grad_scale
    bias_grad = lax.optimization_barrier(jnp.sum(preact_grad.astype(jnp.float32), axis=0)) * grad_scale
    hidden_grad = lax.dot_general(preact_grad, weight, (((1,), (1,)), ((), ())), preferred_element_type=jnp.float32).astype(jnp.bfloat16)
    grad_tiles = hidden_grad.reshape(node_total // TILE, TILE, HID)

    def back_step(running, tile_index):
        source_index, active = tile_meta(tile_index)
        contrib = jnp.einsum('kij,if->kjf', tile_values[tile_index].astype(jnp.float32), grad_tiles[tile_index].astype(jnp.float32))
        contrib = contrib * active[:, None, None]
        return (running.at[source_index].add(contrib), None)
    start_value = jnp.zeros((node_total // TILE, TILE, HID), jnp.float32)
    summed, _ = lax.scan(back_step, start_value, tile_range)
    feature_grad = summed.reshape(node_total, HID).astype(jnp.bfloat16)
    return (layer_out, feature_grad, weight_grad, bias_grad)
```

```python
import functools
import math

import jax
import jax.numpy as jnp
import numpy as np
from jax import lax
from jax.experimental import pallas as pl
from jax.experimental.pallas import tpu as pltpu
from jax.sharding import PartitionSpec as P

BF16 = jnp.bfloat16
F32 = jnp.float32
GROUP = 4
DEPTH = 4

VMEM = pl.BlockSpec(memory_space=pltpu.VMEM)
SMEM = pl.BlockSpec(memory_space=pltpu.SMEM)
HBM = pl.BlockSpec(memory_space=pl.ANY)


def ring_order(count):
    return list(range(0, count, 2)) + list(range(count - 1, 0, -2))


def params(mib):
    return pltpu.CompilerParams(vmem_limit_bytes=mib * 2**20)


def cost(flops, nbytes):
    return pl.CostEstimate(flops=int(flops), bytes_accessed=int(nbytes), transcendentals=0)


def lists_kernel(slots, far, cols, counts, place, pos_of, fwd, bwd, groups):
    row_tiles = pos_of.shape[0]
    col_tiles = place.shape[0]
    cap_f = fwd.shape[0] // 2
    cap_b = bwd.shape[0] // col_tiles

    def clear(k, _):
        groups[2 + k] = 0
        return 0

    lax.fori_loop(0, col_tiles, clear, 0)

    def tile_row(t, filled):
        pos = pos_of[t]

        def slot(s, filled):
            near_n, far_n = filled
            k = place[cols[t * slots + s]]
            head = (t * slots + s) * 65536 + pos * 256
            is_far = (k >= far).astype(jnp.int32)
            at = jnp.where(k >= far, cap_f + far_n, near_n)
            fwd[at] = head + k - is_far * far
            count = groups[2 + k]
            bwd[k * cap_b + count] = head
            groups[2 + k] = count + 1
            return near_n + 1 - is_far, far_n + is_far

        near_n, far_n = lax.fori_loop(0, counts[t], slot, filled)
        head = t * slots * 65536 + pos * 256
        near_top = (near_n + GROUP - 1) // GROUP * GROUP
        far_top = (far_n + GROUP - 1) // GROUP * GROUP

        def fill_near(i, _):
            fwd[i] = head + far
            return 0

        def fill_far(i, _):
            fwd[cap_f + i] = head + col_tiles - far
            return 0

        lax.fori_loop(near_n, near_top, fill_near, 0)
        lax.fori_loop(far_n, far_top, fill_far, 0)
        return near_top, far_top

    near_n, far_n = lax.fori_loop(0, row_tiles, tile_row, (0, 0))
    groups[0] = near_n // GROUP
    groups[1] = far_n // GROUP

    def fill_bwd(k, _):
        count = groups[2 + k]
        top = (count + GROUP - 1) // GROUP * GROUP

        def fill(i, _):
            bwd[k * cap_b + i] = row_tiles * 256
            return 0

        lax.fori_loop(count, top, fill, 0)
        groups[2 + k] = top // GROUP
        return 0

    lax.fori_loop(0, col_tiles, fill_bwd, 0)


def make_lists(tile_cols, tile_counts, place, pos_of, far):
    row_tiles, slots = tile_cols.shape
    col_tiles = place.shape[0]
    cap_f = row_tiles * (slots + GROUP)
    cap_b = row_tiles * slots + GROUP
    i32 = lambda n: jax.ShapeDtypeStruct((n,), jnp.int32)
    return pl.pallas_call(
        functools.partial(lists_kernel, slots, far),
        in_specs=[SMEM] * 4,
        out_specs=[SMEM] * 3,
        out_shape=[i32(2 * cap_f), i32(col_tiles * cap_b), i32(2 + col_tiles)],
        cost_estimate=cost(0, 2**22),
        name="lists",
    )(tile_cols.reshape(-1), tile_counts.reshape(-1), place, pos_of)


def tile_copy(entry, values, buffer, sems, at):
    return pltpu.make_async_copy(values.at[entry // 65536], buffer.at[at], sems.at[at])


def start_group(list_ref, base, g, values, buffer, sems):
    for u in range(GROUP):
        at = lax.rem(g, DEPTH) * GROUP + u
        tile_copy(list_ref[base + g * GROUP + u], values, buffer, sems, at).start()


def wait_group(list_ref, base, g, values, buffer, sems):
    for u in range(GROUP):
        at = lax.rem(g, DEPTH) * GROUP + u
        tile_copy(list_ref[base + g * GROUP + u], values, buffer, sems, at).wait()


def stream(list_ref, base, count, values, buffer, sems, use):
    def ahead(g, _):
        start_group(list_ref, base, g, values, buffer, sems)
        return 0

    lax.fori_loop(0, jnp.minimum(count, DEPTH - 1), ahead, 0)

    def step(g, _):
        @pl.when(g + DEPTH - 1 < count)
        def _():
            start_group(list_ref, base, g + DEPTH - 1, values, buffer, sems)

        wait_group(list_ref, base, g, values, buffer, sems)
        use(base + g * GROUP, lax.rem(g, DEPTH) * GROUP)
        return 0

    lax.fori_loop(0, count, step, 0)


def forward_near_kernel(n_blocks, fwd, groups, values, *refs):
    blocks, (total, source, buffer, sems, block_sems) = refs[:n_blocks], refs[n_blocks:]
    tiles_each = blocks[0].shape[0]
    copies = [
        pltpu.make_async_copy(b, source.at[pl.ds(i * tiles_each, tiles_each)], block_sems.at[i])
        for i, b in enumerate(blocks)
    ]
    for c in copies:
        c.start()
    source[n_blocks * tiles_each] = jnp.zeros(source.shape[1:], BF16)
    total[...] = jnp.zeros(total.shape, F32)
    for c in copies:
        c.wait()

    def use(first, at):
        pos = lax.rem(fwd[first] // 256, 256)
        added = None
        for u in range(GROUP):
            k = lax.rem(fwd[first + u], 256)
            part = jnp.dot(buffer[at + u], source[k], preferred_element_type=F32)
            added = part if added is None else added + part
        total[pos] += added

    stream(fwd, 0, groups[0], values, buffer, sems, use)


def forward_far_kernel(cap_f, fwd, groups, values, before, near, away, mine, other, total, source, buffer, sems, block_sems):
    half = near.shape[0]
    copies = [
        pltpu.make_async_copy(near, source.at[pl.ds(0, half)], block_sems.at[0]),
        pltpu.make_async_copy(away, source.at[pl.ds(half, half)], block_sems.at[1]),
        pltpu.make_async_copy(before, total, block_sems.at[2]),
    ]
    for c in copies:
        c.start()
    source[2 * half] = jnp.zeros(source.shape[1:], BF16)
    for c in copies:
        c.wait()

    def use(first, at):
        pos = lax.rem(fwd[first] // 256, 256)
        added = None
        for u in range(GROUP):
            k = lax.rem(fwd[first + u], 256)
            part = jnp.dot(buffer[at + u], source[k], preferred_element_type=F32)
            added = part if added is None else added + part
        total[pos] += added

    stream(fwd, cap_f, groups[1], values, buffer, sems, use)
    half_rows = mine.shape[0]
    mine[...] = total[:half_rows].astype(BF16)
    other[...] = total[half_rows:].astype(BF16)


def dense_kernel(own, came, weight, bias, cot_own, cot_other, out, grad_t, wgrad):
    tile = grad_t.shape[1]
    half = out.shape[0]
    tiles_half = half // tile
    w = weight[...]
    b = bias[...]
    wg = None
    bg = None
    for h in range(2):
        near = own[h * tiles_half : (h + 1) * tiles_half].reshape(half, -1).astype(F32)
        away = came[(1 - h) * tiles_half : (2 - h) * tiles_half].reshape(half, -1).astype(F32)
        hidden = (near + away).astype(BF16)
        preact = jnp.dot(hidden, w, preferred_element_type=F32) + b
        sig = 1.0 / (1.0 + jnp.exp(-preact))
        cot = (cot_own if h == 0 else cot_other)[...].astype(F32)
        if h == 0:
            out[...] = (preact * sig).astype(BF16)
        pgrad = (cot * (sig * (1.0 + preact * (1.0 - sig)))).astype(BF16)
        for i in range(tiles_half):
            rows = pgrad[i * tile : (i + 1) * tile]
            grad_t[h * tiles_half + i] = lax.dot_general(
                w, rows, (((1,), (1,)), ((), ())), preferred_element_type=F32
            ).astype(BF16)
        part = lax.dot_general(hidden, pgrad, (((0,), (0,)), ((), ())), preferred_element_type=F32)
        bias_part = jnp.sum(pgrad.astype(F32), axis=0, keepdims=True)
        wg = part if wg is None else wg + part
        bg = bias_part if bg is None else bg + bias_part
    rows = wg.shape[0] // 4
    for q in range(4):
        wgrad[q, :rows] = wg[q * rows : (q + 1) * rows]
        wgrad[q, rows:] = jnp.broadcast_to(bg, (wgrad.shape[1] - rows, bg.shape[1]))


def backward_kernel(ks, cap_b, bwd, groups, values, grad_mine, grad_came, out, grads, buffer, sems, block_sems):
    half = grad_mine.shape[0]
    copies = [
        pltpu.make_async_copy(grad_mine, grads.at[pl.ds(0, half)], block_sems.at[0]),
        pltpu.make_async_copy(grad_came, grads.at[pl.ds(half, half)], block_sems.at[1]),
    ]
    for c in copies:
        c.start()
    grads[2 * half] = jnp.zeros(grads.shape[1:], BF16)
    out[...] = jnp.zeros(out.shape, F32)
    for c in copies:
        c.wait()
    for i, k in enumerate(ks):

        def use(first, at, i=i):
            added = None
            for u in range(GROUP):
                pos = lax.rem(bwd[first + u] // 256, 256)
                part = jnp.dot(grads[pos], buffer[at + u], preferred_element_type=F32)
                added = part if added is None else added + part
            out[i] += added

        stream(bwd, k * cap_b, groups[2 + k], values, buffer, sems, use)


def finish_kernel(own, right, left, out):
    tiles, _, tile = own.shape
    for i in range(tiles):
        total = own[i] + right[i].astype(F32) + left[i].astype(F32)
        out[i * tile : (i + 1) * tile] = total.T.astype(BF16)


def per_device(n_col, features, tile_values, tile_cols, tile_counts, weight, bias, cotangent):
    node_dev, width = features.shape
    row_tiles, slots, tile, _ = tile_values.shape
    per_dev = node_dev // tile
    col_tiles = n_col * per_dev
    half = n_col // 2
    far = col_tiles - per_dev
    node_total = node_dev * lax.axis_size("row") * n_col
    grad_scale = 1.0 / math.sqrt(node_total)
    values = tile_values.reshape(row_tiles * slots, tile, tile)

    order = ring_order(n_col)
    right = [(order[i], order[(i + 1) % n_col]) for i in range(n_col)]
    left = [(b, a) for a, b in right]
    cores = [(0, 1), (1, 0), (2, 3), (3, 2)]
    across = [(0, 2), (2, 0), (1, 3), (3, 1)]
    row = lax.axis_index("row")
    col = lax.axis_index("col")
    my_y, my_core = row // 2, row % 2

    rank = np.zeros(n_col, np.int32)
    rank[order] = np.arange(n_col)
    steps = np.arange(n_col)
    arrival_of_step = np.where(steps == 0, 0, np.where(steps < half, 2 * steps, np.where(steps == half, n_col - 1, 2 * (n_col - steps) - 1)))
    table = np.zeros((n_col, col_tiles), np.int32)
    for d in range(n_col):
        for t in range(col_tiles):
            ahead = (rank[t // per_dev] - rank[d]) % n_col
            table[d, t] = arrival_of_step[ahead] * per_dev + t % per_dev
    place = lax.dynamic_index_in_dim(jnp.asarray(table), col, 0, keepdims=False)
    tiles = np.arange(row_tiles)
    tiles_r = row_tiles // 4
    pos_table = np.zeros((4, row_tiles), np.int32)
    for r in range(4):
        block = tiles // tiles_r
        pos_table[r] = ((block % 2 != r % 2) * 2 + (block // 2 != r // 2)) * tiles_r + tiles % tiles_r
    pos_of = lax.dynamic_index_in_dim(jnp.asarray(pos_table), row, 0, keepdims=False)

    fwd, bwd, groups = make_lists(tile_cols, tile_counts, place, pos_of, far)
    cap_f = fwd.shape[0] // 2
    cap_b = bwd.shape[0] // col_tiles

    mine = features.reshape(per_dev, tile, width)
    arrived = [mine]
    from_left = from_right = mine
    for _ in range(half - 1):
        from_left = lax.ppermute(from_left, "col", right)
        from_right = lax.ppermute(from_right, "col", left)
        arrived += [from_left, from_right]
    far_near = lax.ppermute(from_left[: per_dev // 2], "col", right)
    far_away = lax.ppermute(from_right[per_dev // 2 :], "col", left)
    cot_other = lax.ppermute(cotangent, "row", across)

    stream_scratch = [pltpu.VMEM((DEPTH * GROUP, tile, tile), BF16), pltpu.SemaphoreType.DMA((DEPTH * GROUP,))]
    dots = 2 * tile * tile * width
    total = pl.pallas_call(
        functools.partial(forward_near_kernel, len(arrived)),
        in_specs=[SMEM, SMEM, HBM] + [HBM] * len(arrived),
        out_specs=VMEM,
        out_shape=jax.ShapeDtypeStruct((row_tiles, tile, width), F32),
        scratch_shapes=[pltpu.VMEM((far + 1, tile, width), BF16)]
        + stream_scratch
        + [pltpu.SemaphoreType.DMA((len(arrived),))],
        compiler_params=params(40),
        cost_estimate=cost(64 * dots, 64 * tile * tile * 2),
        name="forward_near",
    )(fwd, groups, values, *arrived)
    half_shape = (row_tiles // 2, tile, width)
    hid_mine, hid_other = pl.pallas_call(
        functools.partial(forward_far_kernel, cap_f),
        in_specs=[SMEM, SMEM, HBM, HBM, HBM, HBM],
        out_specs=[VMEM, VMEM],
        out_shape=[jax.ShapeDtypeStruct(half_shape, BF16)] * 2,
        scratch_shapes=[pltpu.VMEM((row_tiles, tile, width), F32), pltpu.VMEM((per_dev + 1, tile, width), BF16)]
        + stream_scratch
        + [pltpu.SemaphoreType.DMA((3,))],
        compiler_params=params(40),
        cost_estimate=cost(16 * dots, 16 * tile * tile * 2),
        name="forward_far",
    )(fwd, groups, values, total, far_near, far_away)

    hid_came = lax.ppermute(hid_other, "row", cores)
    own = (hid_mine.astype(F32) + hid_came.astype(F32)).astype(BF16)
    came = lax.ppermute(own, "row", across)

    q_rows = width // 4 + 8
    layer_out, grad_mine, wgrad = pl.pallas_call(
        dense_kernel,
        in_specs=[VMEM] * 6,
        out_specs=[VMEM] * 3,
        out_shape=[
            jax.ShapeDtypeStruct((node_dev, width), BF16),
            jax.ShapeDtypeStruct((row_tiles // 2, width, tile), BF16),
            jax.ShapeDtypeStruct((4, q_rows, width), F32),
        ],
        compiler_params=params(40),
        cost_estimate=cost(3 * 2 * 2 * node_dev * width * width, 8 * node_dev * width),
        name="dense",
    )(own, came, weight, bias.reshape(1, -1), cotangent, cot_other)
    grad_came = lax.ppermute(grad_mine, "row", cores)

    wgrad = wgrad.reshape(2, 2, q_rows, width)
    part = lax.dynamic_index_in_dim(wgrad, my_core, 0, keepdims=False)
    part = part + lax.ppermute(lax.dynamic_index_in_dim(wgrad, 1 - my_core, 0, keepdims=False), "row", cores)
    part = lax.dynamic_index_in_dim(part, my_y, 0, keepdims=False)
    wsum, w_left, w_right = part, part, part
    for s in range(half):
        w_left = lax.ppermute(w_left, "col", right)
        wsum = wsum + w_left
        if s < half - 1:
            w_right = lax.ppermute(w_right, "col", left)
            wsum = wsum + w_right
    wsum = wsum * grad_scale
    w_y = lax.ppermute(wsum, "row", across)
    pair = jnp.where(my_y == 0, jnp.stack([wsum, w_y]), jnp.stack([w_y, wsum]))
    w_c = lax.ppermute(pair, "row", cores)
    quads = jnp.where(my_core == 0, jnp.stack([pair, w_c]), jnp.stack([w_c, pair]))
    quads = quads.reshape(4, q_rows, width)
    weight_grad = quads[:, : width // 4].reshape(width, width)
    bias_grad = quads[0, width // 4]

    def backward(ks, name):
        return pl.pallas_call(
            functools.partial(backward_kernel, ks, cap_b),
            in_specs=[SMEM, SMEM, HBM, HBM, HBM],
            out_specs=VMEM,
            out_shape=jax.ShapeDtypeStruct((len(ks), width, tile), F32),
            scratch_shapes=[pltpu.VMEM((row_tiles + 1, width, tile), BF16)]
            + stream_scratch
            + [pltpu.SemaphoreType.DMA((2,))],
            compiler_params=params(40),
            cost_estimate=cost(16 * dots, 16 * tile * tile * 2),
            name=name,
        )(bwd, groups, values, grad_mine, grad_came)

    def block(arrival):
        return [arrival * per_dev + i for i in range(per_dev)]

    far_part = backward(block(n_col - 1), "backward_far").astype(BF16)
    to_right = lax.ppermute(far_part[: per_dev // 2], "col", right)
    to_left = lax.ppermute(far_part[per_dev // 2 :], "col", left)
    for d in range(half - 1, 0, -1):
        both = backward(block(2 * d) + block(2 * d - 1), "backward")
        for_right, for_left = both[:per_dev], both[per_dev:]
        if d == half - 1:
            zeros = jnp.zeros((per_dev - per_dev // 2, width, tile), BF16)
            to_right = jnp.concatenate([to_right, zeros])
            to_left = jnp.concatenate([jnp.zeros((per_dev // 2, width, tile), BF16), to_left])
        to_right = lax.ppermute((for_right + to_right.astype(F32)).astype(BF16), "col", right)
        to_left = lax.ppermute((for_left + to_left.astype(F32)).astype(BF16), "col", left)
    own_part = backward(block(0), "backward_own")
    feature_grad = pl.pallas_call(
        finish_kernel,
        in_specs=[VMEM] * 3,
        out_specs=VMEM,
        out_shape=jax.ShapeDtypeStruct((node_dev, width), BF16),
        name="finish",
    )(own_part, to_right, to_left)
    return (layer_out, feature_grad, weight_grad, bias_grad)


def solution(mesh):
    placed = (
        P(("row", "col"), None),
        P("col", "row", None, None),
        P("col", "row"),
        P("col", "row"),
        P(),
        P(),
        P(("col", "row"), None),
    )
    return jax.shard_map(
        functools.partial(per_device, mesh.shape["col"]),
        mesh=mesh,
        in_specs=placed,
        out_specs=(P(("col", "row"), None), P(("row", "col"), None), P(), P()),
        check_vma=False,
    )
```

```python
import functools
import math

import jax
import jax.numpy as jnp
import numpy as np
from jax import lax
from jax.experimental import pallas as pl
from jax.experimental.pallas import tpu as pltpu
from jax.sharding import PartitionSpec as P

BF16 = jnp.bfloat16
F32 = jnp.float32
GROUP = 4
FWD_GROUPS = (4, 4, 2)
DEPTH = 8

VMEM = pl.BlockSpec(memory_space=pltpu.VMEM)
SMEM = pl.BlockSpec(memory_space=pltpu.SMEM)
HBM = pl.BlockSpec(memory_space=pl.ANY)


def ring_order(count):
    return list(range(0, count, 2)) + list(range(count - 1, 0, -2))


def params(mib):
    return pltpu.CompilerParams(vmem_limit_bytes=mib * 2**20)


def cost(flops, nbytes):
    return pl.CostEstimate(flops=int(flops), bytes_accessed=int(nbytes), transcendentals=0)


def round_up(n, step):
    return (n + step - 1) // step * step


def lists_kernel(slots, cuts, cols, counts, place, pos_of, fwd, bwd, groups):
    row_tiles = pos_of.shape[0]
    col_tiles = place.shape[0]
    passes = len(cuts) - 1
    cap_f = fwd.shape[0] // passes
    cap_b = bwd.shape[0] // col_tiles

    def clear(k, _):
        groups[passes + k] = 0
        return 0

    lax.fori_loop(0, col_tiles, clear, 0)

    def tile_row(t, filled):
        pos = pos_of[t]

        def slot(s, filled):
            k = place[cols[t * slots + s]]
            head = (t * slots + s) * 65536 + pos * 256
            at = filled[0]
            first = 0
            for p in range(1, passes):
                at = jnp.where(k >= cuts[p], p * cap_f + filled[p], at)
                first = jnp.where(k >= cuts[p], cuts[p], first)
            fwd[at] = head + k - first
            count = groups[passes + k]
            bwd[k * cap_b + count] = head
            groups[passes + k] = count + 1
            return tuple(
                n + ((k >= cuts[p]) & (k < cuts[p + 1])).astype(jnp.int32) for p, n in enumerate(filled)
            )

        filled = lax.fori_loop(0, counts[t], slot, filled)
        head = t * slots * 65536 + pos * 256
        tops = []
        for p, n in enumerate(filled):
            top = round_up(n, FWD_GROUPS[p])

            def fill(i, _, p=p):
                fwd[p * cap_f + i] = head + cuts[p + 1] - cuts[p]
                return 0

            lax.fori_loop(n, top, fill, 0)
            tops.append(top)
        return tuple(tops)

    filled = lax.fori_loop(0, row_tiles, tile_row, (0,) * passes)
    for p in range(passes):
        groups[p] = filled[p] // FWD_GROUPS[p]

    def fill_bwd(k, _):
        count = groups[passes + k]
        top = round_up(count, GROUP)

        def fill(i, _):
            bwd[k * cap_b + i] = row_tiles * 256
            return 0

        lax.fori_loop(count, top, fill, 0)
        groups[passes + k] = top // GROUP
        return 0

    lax.fori_loop(0, col_tiles, fill_bwd, 0)


def make_lists(tile_cols, tile_counts, place, pos_of, cuts):
    row_tiles, slots = tile_cols.shape
    col_tiles = place.shape[0]
    passes = len(cuts) - 1
    cap_f = row_tiles * (slots + GROUP)
    cap_b = row_tiles * slots + GROUP
    i32 = lambda n: jax.ShapeDtypeStruct((n,), jnp.int32)
    return pl.pallas_call(
        functools.partial(lists_kernel, slots, cuts),
        in_specs=[SMEM] * 4,
        out_specs=[SMEM] * 3,
        out_shape=[i32(passes * cap_f), i32(col_tiles * cap_b), i32(passes + col_tiles)],
        compiler_params=params(8),
        cost_estimate=cost(0, 2**22),
        name="lists",
    )(tile_cols.reshape(-1), tile_counts.reshape(-1), place, pos_of)


def stream(list_ref, segments, size, values, buffer, sems, between, use):
    depth = buffer.shape[0] // size
    ends = []
    for _, n in segments:
        ends.append(n + (ends[-1] if ends else 0))
    total = ends[-1]

    def locate(g):
        segment, first = 0, segments[0][0] + g * size
        for i in range(1, len(segments)):
            past = g >= ends[i - 1]
            segment = jnp.where(past, i, segment)
            first = jnp.where(past, segments[i][0] + (g - ends[i - 1]) * size, first)
        return segment, first

    def copies(g):
        _, first = locate(g)
        at = lax.rem(g, depth) * size
        for u in range(size):
            yield pltpu.make_async_copy(values.at[list_ref[first + u] // 65536], buffer.at[at + u], sems.at[at + u])

    def ahead(g, _):
        for c in copies(g):
            c.start()
        return 0

    lax.fori_loop(0, jnp.minimum(total, depth - 1), ahead, 0)
    between()

    def step(g, _):
        @pl.when(g + depth - 1 < total)
        def _():
            ahead(g + depth - 1, 0)

        for c in copies(g):
            c.wait()
        segment, first = locate(g)
        use(segment, first, lax.rem(g, depth) * size)
        return 0

    lax.fori_loop(0, total, step, 0)


def forward_kernel(p, cap_f, n_blocks, n_before, last, fwd, groups, values, *refs):
    blocks, refs = refs[:n_blocks], refs[n_blocks:]
    before, refs = refs[:n_before], refs[n_before:]
    outs, (total, source, buffer, sems, block_sems) = refs[:-5], refs[-5:]
    size = FWD_GROUPS[p]
    copies = []
    at = 0
    for i, b in enumerate(blocks):
        copies.append(pltpu.make_async_copy(b, source.at[pl.ds(at, b.shape[0])], block_sems.at[i]))
        at += b.shape[0]

    def between():
        for c in copies:
            c.start()
        source[at] = jnp.zeros(source.shape[1:], BF16)
        total[...] = jnp.zeros(total.shape, F32)
        for c in copies:
            c.wait()

    def use(segment, first, at):
        pos = lax.rem(fwd[first] // 256, 256)
        added = None
        for u in range(size):
            k = lax.rem(fwd[first + u], 256)
            part = jnp.dot(buffer[at + u], source[k], preferred_element_type=F32)
            added = part if added is None else added + part
        total[pos] += added

    stream(fwd, [(p * cap_f, groups[p])], size, values, buffer, sems, between, use)
    row_tiles = total.shape[0]
    for i in range(row_tiles):
        done = total[i]
        for b in before:
            done = done + b[i]
        if last:
            mine, other = outs
            if i < row_tiles // 2:
                mine[i] = done.astype(BF16)
            else:
                other[i - row_tiles // 2] = done.astype(BF16)
        else:
            outs[0][i] = done


def dense_kernel(own, came, weight, bias, cot_own, cot_other, out, grad_t, wgrad):
    tile = grad_t.shape[1]
    half = out.shape[0]
    tiles_half = half // tile
    w = weight[...]
    b = bias[...]
    wg = None
    bg = None
    for h in range(2):
        near = own[h * tiles_half : (h + 1) * tiles_half].reshape(half, -1).astype(F32)
        away = came[(1 - h) * tiles_half : (2 - h) * tiles_half].reshape(half, -1).astype(F32)
        hidden = (near + away).astype(BF16)
        preact = jnp.dot(hidden, w, preferred_element_type=F32) + b
        sig = 1.0 / (1.0 + jnp.exp(-preact))
        cot = (cot_own if h == 0 else cot_other)[...].astype(F32)
        if h == 0:
            out[...] = (preact * sig).astype(BF16)
        pgrad = (cot * (sig * (1.0 + preact * (1.0 - sig)))).astype(BF16)
        for i in range(tiles_half):
            rows = pgrad[i * tile : (i + 1) * tile]
            grad_t[h * tiles_half + i] = lax.dot_general(
                w, rows, (((1,), (1,)), ((), ())), preferred_element_type=F32
            ).astype(BF16)
        part = lax.dot_general(hidden, pgrad, (((0,), (0,)), ((), ())), preferred_element_type=F32)
        bias_part = jnp.sum(pgrad.astype(F32), axis=0, keepdims=True)
        wg = part if wg is None else wg + part
        bg = bias_part if bg is None else bg + bias_part
    rows = wg.shape[0] // 2
    for q in range(2):
        wgrad[q, :rows] = wg[q * rows : (q + 1) * rows]
        wgrad[q, rows:] = jnp.broadcast_to(bg, (wgrad.shape[1] - rows, bg.shape[1]))


def backward_kernel(ks, passes, cap_b, bwd, groups, values, grad_mine, grad_came, out, grads, buffer, sems, block_sems):
    half = grad_mine.shape[0]
    copies = [
        pltpu.make_async_copy(grad_mine, grads.at[pl.ds(0, half)], block_sems.at[0]),
        pltpu.make_async_copy(grad_came, grads.at[pl.ds(half, half)], block_sems.at[1]),
    ]

    def between():
        for c in copies:
            c.start()
        grads[2 * half] = jnp.zeros(grads.shape[1:], BF16)
        out[...] = jnp.zeros(out.shape, F32)
        for c in copies:
            c.wait()

    def use(segment, first, at):
        added = None
        for u in range(GROUP):
            pos = lax.rem(bwd[first + u] // 256, 256)
            part = jnp.dot(grads[pos], buffer[at + u], preferred_element_type=F32)
            added = part if added is None else added + part
        out[segment] += added

    segments = [(k * cap_b, groups[passes + k]) for k in ks]
    stream(bwd, segments, GROUP, values, buffer, sems, between, use)


def finish_kernel(own, right, left, out):
    tiles, _, tile = own.shape
    for i in range(tiles):
        rows = pl.ds(i * tile, tile)
        total = own[i] + right[rows, :].astype(F32) + left[rows, :].astype(F32)
        out[rows, :] = total.T.astype(BF16)


def per_device(n_col, features, tile_values, tile_cols, tile_counts, weight, bias, cotangent):
    node_dev, width = features.shape
    row_tiles, slots, tile, _ = tile_values.shape
    per_dev = node_dev // tile
    col_tiles = n_col * per_dev
    half = n_col // 2
    far = col_tiles - per_dev
    node_total = node_dev * lax.axis_size("row") * n_col
    grad_scale = 1.0 / math.sqrt(node_total)
    values = tile_values.reshape(row_tiles * slots, tile, tile)

    order = ring_order(n_col)
    right = [(order[i], order[(i + 1) % n_col]) for i in range(n_col)]
    left = [(b, a) for a, b in right]
    cores = [(0, 1), (1, 0), (2, 3), (3, 2)]
    across = [(0, 2), (2, 0), (1, 3), (3, 1)]
    row = lax.axis_index("row")
    col = lax.axis_index("col")
    my_y, my_core = row // 2, row % 2

    rank = np.zeros(n_col, np.int32)
    rank[order] = np.arange(n_col)
    steps = np.arange(n_col)
    arrival_of_step = np.where(steps == 0, 0, np.where(steps < half, 2 * steps, np.where(steps == half, n_col - 1, 2 * (n_col - steps) - 1)))
    table = np.zeros((n_col, col_tiles), np.int32)
    for d in range(n_col):
        for t in range(col_tiles):
            ahead = (rank[t // per_dev] - rank[d]) % n_col
            table[d, t] = arrival_of_step[ahead] * per_dev + t % per_dev
    place = lax.dynamic_index_in_dim(jnp.asarray(table), col, 0, keepdims=False)
    tiles = np.arange(row_tiles)
    tiles_r = row_tiles // 4
    pos_table = np.zeros((4, row_tiles), np.int32)
    for r in range(4):
        block = tiles // tiles_r
        pos_table[r] = ((block % 2 != r % 2) * 2 + (block // 2 != r // 2)) * tiles_r + tiles % tiles_r
    pos_of = lax.dynamic_index_in_dim(jnp.asarray(pos_table), row, 0, keepdims=False)

    cuts = (0, far - 2 * per_dev, far, col_tiles)
    passes = len(cuts) - 1
    fwd, bwd, groups = make_lists(tile_cols, tile_counts, place, pos_of, cuts)
    cap_f = fwd.shape[0] // passes
    cap_b = bwd.shape[0] // col_tiles

    stream_scratch = [pltpu.VMEM((DEPTH * GROUP, tile, tile), BF16), pltpu.SemaphoreType.DMA((DEPTH * GROUP,))]
    dots = 2 * tile * tile * width
    total_shape = jax.ShapeDtypeStruct((row_tiles, tile, width), F32)
    half_shape = jax.ShapeDtypeStruct((row_tiles // 2, tile, width), BF16)

    def forward(p, blocks, before, last=False):
        n_tiles = sum(b.shape[0] for b in blocks)
        return pl.pallas_call(
            functools.partial(forward_kernel, p, cap_f, len(blocks), len(before), last),
            in_specs=[SMEM, SMEM, HBM] + [HBM] * len(blocks) + [VMEM] * len(before),
            out_specs=[VMEM] * (2 if last else 1),
            out_shape=[half_shape] * 2 if last else [total_shape],
            scratch_shapes=[pltpu.VMEM(total_shape.shape, F32), pltpu.VMEM((n_tiles + 1, tile, width), BF16)]
            + stream_scratch
            + [pltpu.SemaphoreType.DMA((len(blocks),))],
            compiler_params=params(40),
            cost_estimate=cost(4 * n_tiles * dots, 4 * n_tiles * tile * tile * 2),
            name=f"forward_{p}",
        )(fwd, groups, values, *blocks, *before)

    mine = features.reshape(per_dev, tile, width)
    arrived = [mine]
    from_left = from_right = mine
    cot_other = None
    for s in range(1, half):
        from_left = lax.ppermute(from_left, "col", right)
        from_right = lax.ppermute(from_right, "col", left)
        if s == 1:
            cot_other = lax.ppermute(cotangent, "row", across)
            from_left, from_right, cot_other, fwd, bwd, groups = lax.optimization_barrier(
                (from_left, from_right, cot_other, fwd, bwd, groups)
            )
        if s == half - 1:
            (total,) = forward(0, arrived, [])
            from_left, from_right, total = lax.optimization_barrier((from_left, from_right, total))
        arrived += [from_left, from_right]
    far_near = lax.ppermute(from_left[: per_dev // 2], "col", right)
    far_away = lax.ppermute(from_right[per_dev // 2 :], "col", left)
    (total,) = forward(1, arrived[-2:], [total])
    hid_mine, hid_other = forward(2, [far_near, far_away], [total], last=True)

    hid_came = lax.ppermute(hid_other, "row", cores)
    own = (hid_mine.astype(F32) + hid_came.astype(F32)).astype(BF16)
    came = lax.ppermute(own, "row", across)

    w_rows = width // 2 + 16
    layer_out, grad_mine, wgrad = pl.pallas_call(
        dense_kernel,
        in_specs=[VMEM] * 6,
        out_specs=[VMEM] * 3,
        out_shape=[
            jax.ShapeDtypeStruct((node_dev, width), BF16),
            jax.ShapeDtypeStruct((row_tiles // 2, width, tile), BF16),
            jax.ShapeDtypeStruct((2, w_rows, width), F32),
        ],
        compiler_params=params(40),
        cost_estimate=cost(3 * 2 * 2 * node_dev * width * width, 8 * node_dev * width),
        name="dense",
    )(own, came, weight, bias.reshape(1, -1), cotangent, cot_other)
    grad_came = lax.ppermute(grad_mine, "row", cores)

    w_came = lax.ppermute(lax.dynamic_index_in_dim(wgrad, 1 - my_core, 0, keepdims=False), "row", cores)
    w_own = (lax.dynamic_index_in_dim(wgrad, my_core, 0, keepdims=False) + w_came).astype(BF16)
    wsum = w_own.astype(F32)

    def backward(ks, name):
        return pl.pallas_call(
            functools.partial(backward_kernel, ks, passes, cap_b),
            in_specs=[SMEM, SMEM, HBM, HBM, HBM],
            out_specs=VMEM,
            out_shape=jax.ShapeDtypeStruct((len(ks), width, tile), F32),
            scratch_shapes=[pltpu.VMEM((row_tiles + 1, width, tile), BF16)]
            + stream_scratch
            + [pltpu.SemaphoreType.DMA((2,))],
            compiler_params=params(40),
            cost_estimate=cost(16 * dots, 16 * tile * tile * 2),
            name=name,
        )(bwd, groups, values, grad_mine, grad_came)

    def block(arrival):
        return [arrival * per_dev + i for i in range(per_dev)]

    far_part = backward(block(n_col - 1), "backward_far").astype(BF16).reshape(node_dev, width)
    cut = per_dev // 2 * tile
    rest = node_dev - cut
    to_right = lax.ppermute(jnp.concatenate([far_part[:cut], w_own]), "col", right)
    to_left = lax.ppermute(jnp.concatenate([far_part[cut:], w_own]), "col", left)
    for d in range(half - 1, 0, -1):
        both = backward(block(2 * d) + block(2 * d - 1), "backward").reshape(2, node_dev, width)
        for_right, for_left = both[0], both[1]
        w_right, w_left = to_right[-w_rows:], to_left[-w_rows:]
        wsum = wsum + w_right.astype(F32) + w_left.astype(F32)
        if d == half - 1:
            add_right = (for_right[:cut] + to_right[:cut].astype(F32)).astype(BF16)
            to_right = jnp.concatenate([add_right, for_right[cut:].astype(BF16), w_right])
            add_left = (for_left[cut:] + to_left[:rest].astype(F32)).astype(BF16)
            to_left = jnp.concatenate([for_left[:cut].astype(BF16), add_left, w_left])
        else:
            add_right = (for_right + to_right[:node_dev].astype(F32)).astype(BF16)
            to_right = lax.dynamic_update_slice(to_right, add_right, (0, 0))
            add_left = (for_left + to_left[:node_dev].astype(F32)).astype(BF16)
            to_left = lax.dynamic_update_slice(to_left, add_left, (0, 0)) if d > 1 else add_left
        to_right = lax.ppermute(to_right, "col", right)
        to_left = lax.ppermute(to_left, "col", left)
    own_part = backward(block(0), "backward_own")
    wsum = (wsum + to_right[-w_rows:].astype(F32)) * grad_scale
    w_half = wsum[: width // 2]
    w_other = lax.ppermute(w_half, "row", cores)
    weight_grad = jnp.where(
        my_core == 0, jnp.concatenate([w_half, w_other]), jnp.concatenate([w_other, w_half])
    )
    bias_grad = wsum[width // 2]
    feature_grad = pl.pallas_call(
        finish_kernel,
        in_specs=[VMEM] * 3,
        out_specs=VMEM,
        out_shape=jax.ShapeDtypeStruct((node_dev, width), BF16),
        compiler_params=params(8),
        name="finish",
    )(own_part, to_right, to_left)
    return (layer_out, feature_grad, weight_grad, bias_grad)


def solution(mesh):
    placed = (
        P(("row", "col"), None),
        P("col", "row", None, None),
        P("col", "row"),
        P("col", "row"),
        P(),
        P(),
        P(("col", "row"), None),
    )
    return jax.shard_map(
        functools.partial(per_device, mesh.shape["col"]),
        mesh=mesh,
        in_specs=placed,
        out_specs=(P(("col", "row"), None), P(("row", "col"), None), P(), P()),
        check_vma=False,
    )
```

```python
import functools
import math

import jax
import jax.numpy as jnp
import numpy as np
from jax import lax
from jax.experimental import pallas as pl
from jax.experimental.pallas import tpu as pltpu
from jax.sharding import PartitionSpec as P

BF16 = jnp.bfloat16
F32 = jnp.float32
UNIT = 8
DEPTH = 5

VMEM = pl.BlockSpec(memory_space=pltpu.VMEM)
SMEM = pl.BlockSpec(memory_space=pltpu.SMEM)
HBM = pl.BlockSpec(memory_space=pltpu.HBM)
ANY = pl.BlockSpec(memory_space=pl.ANY)


def ring_order(count):
    return list(range(0, count, 2)) + list(range(count - 1, 0, -2))


def params(mib):
    return pltpu.CompilerParams(vmem_limit_bytes=mib * 2**20)


def cost(flops, nbytes):
    return pl.CostEstimate(flops=int(flops), bytes_accessed=int(nbytes), transcendentals=0)


def lists_kernel(n_buckets, cap, col_tiles, place_base, cols, counts, tables, lists):
    row_tiles, slots = cols.shape
    ends = n_buckets * cap
    first_place = place_base + lax.axis_index("col") * col_tiles
    first_pos = lax.axis_index("row") * row_tiles
    for b in range(n_buckets):
        lists[ends + b] = 0

    def tile_row(t, _):
        head = t * slots * 65536 + tables[first_pos + t] * 256

        def slot(s, _):
            place = tables[first_place + cols[t, s]]
            bucket = place // 256
            n = lists[ends + bucket]
            lists[bucket * cap + n] = head + s * 65536 + lax.rem(place, 256)
            lists[ends + bucket] = n + 1
            return 0

        lax.fori_loop(0, counts[t], slot, 0)
        return 0

    lax.fori_loop(0, row_tiles, tile_row, 0)
    for b in range(n_buckets):
        n = lists[ends + b]
        units = (n + UNIT - 1) // UNIT

        def fill(i, _, b=b):
            lists[b * cap + i] = row_tiles * 256
            return 0

        lax.fori_loop(n, units * UNIT, fill, 0)
        lists[ends + b] = units


def stream(lists, buckets, cap, n_buckets, values, buffer, sems, between, use):
    ends = []
    for b in buckets:
        n = lists[n_buckets * cap + b]
        ends.append(n + (ends[-1] if ends else 0))
    total = ends[-1]

    def locate(g):
        first = buckets[0] * cap + g * UNIT
        for i in range(1, len(buckets)):
            first = jnp.where(g >= ends[i - 1], buckets[i] * cap + (g - ends[i - 1]) * UNIT, first)
        return first

    def copies(g):
        first = locate(g)
        at = lax.rem(g, DEPTH) * UNIT
        for u in range(UNIT):
            yield pltpu.make_async_copy(values.at[lists[first + u] // 65536], buffer.at[at + u], sems.at[at + u])

    def ahead(g, _):
        for c in copies(g):
            c.start()
        return 0

    lax.fori_loop(0, jnp.minimum(total, DEPTH - 1), ahead, 0)
    between()

    def step(g, _):
        @pl.when(g + DEPTH - 1 < total)
        def _():
            ahead(g + DEPTH - 1, 0)

        for c in copies(g):
            c.wait()
        use(locate(g), lax.rem(g, DEPTH) * UNIT)
        return 0

    lax.fori_loop(0, total, step, 0)


def destination(entry):
    return lax.rem(entry // 256, 256)


def source(entry):
    return lax.rem(entry, 256)


def forward_kernel(buckets, cap, n_buckets, n_blocks, n_before, last, lists, values, *refs):
    blocks, refs = refs[:n_blocks], refs[n_blocks:]
    before, refs = refs[:n_before], refs[n_before:]
    (buffer, sems, block_sems, sources), refs = refs[-4:], refs[:-4]
    total = refs[-1]
    copies = []
    starts = []
    at = 0
    for i, b in enumerate(blocks):
        copies.append(pltpu.make_async_copy(b, sources.at[pl.ds(at, b.shape[0])], block_sems.at[i]))
        starts.append(at)
        at += b.shape[0]

    def between():
        for c in copies:
            c.start()
        if n_before:
            total[...] = before[0][...]
        else:
            total[...] = jnp.zeros(total.shape, F32)
        for c in copies:
            c.wait()

    def use(first, at):
        parts = []
        for u in range(UNIT):
            parts.append(jnp.dot(buffer[at + u], sources[source(lists[first + u])], preferred_element_type=F32))
        for u in range(UNIT):
            total[destination(lists[first + u])] += parts[u]

    stream(lists, buckets, cap, n_buckets, values, buffer, sems, between, use)
    if last:
        mine, other, _ = refs
        half = mine.shape[0]
        mine[...] = total[:half].astype(BF16)
        other[...] = total[half : 2 * half].astype(BF16)


def dense_kernel(second, near, away, weight, bias, cot, *refs):
    if second:
        before, grad_t, wgrad = refs
    else:
        out, grad_t, wgrad = refs
    tiles, tile, width = near.shape
    w = weight[...]
    hidden = near[...].reshape(tiles * tile, width).astype(F32) + away[...].reshape(tiles * tile, width).astype(F32)
    hidden = hidden.astype(BF16)
    preact = jnp.dot(hidden, w, preferred_element_type=F32) + bias[...]
    sig = 1.0 / (1.0 + jnp.exp(-preact))
    if not second:
        out[...] = (preact * sig).astype(BF16)
    pgrad = (cot[...].astype(F32) * (sig * (1.0 + preact * (1.0 - sig)))).astype(BF16)
    for i in range(tiles):
        grad_t[i] = lax.dot_general(
            w, pgrad[i * tile : (i + 1) * tile], (((1,), (1,)), ((), ())), preferred_element_type=F32
        ).astype(BF16)
    wg = lax.dot_general(hidden, pgrad, (((0,), (0,)), ((), ())), preferred_element_type=F32)
    bg = jnp.sum(pgrad.astype(F32), axis=0, keepdims=True)
    if second:
        wg = wg + before[:width]
        bg = bg + before[width : width + 1]
        rows = width // 4
        for q in range(4):
            wgrad[q, :rows] = wg[q * rows : (q + 1) * rows]
            wgrad[q, rows:] = jnp.broadcast_to(bg, (wgrad.shape[1] - rows, width))
    else:
        wgrad[:width] = wg
        wgrad[width:] = jnp.broadcast_to(bg, (wgrad.shape[0] - width, width))


def backward_kernel(bucket, cap, n_buckets, lists, values, *refs):
    parts, (out, grads, buffer, sems, part_sems) = refs[:-5], refs[-5:]
    copies = []
    at = 0
    for i, g in enumerate(parts):
        copies.append(pltpu.make_async_copy(g, grads.at[pl.ds(at, g.shape[0])], part_sems.at[i]))
        at += g.shape[0]

    def between():
        for c in copies:
            c.start()
        grads[at] = jnp.zeros(grads.shape[1:], BF16)
        out[...] = jnp.zeros(out.shape, F32)
        for c in copies:
            c.wait()

    def use(first, at):
        parts = []
        for u in range(UNIT):
            parts.append(jnp.dot(grads[destination(lists[first + u])], buffer[at + u], preferred_element_type=F32))
        for u in range(UNIT):
            out[source(lists[first + u])] += parts[u]

    stream(lists, [bucket], cap, n_buckets, values, buffer, sems, between, use)


def finish_kernel(own, right, left, out):
    tiles, _, tile = own.shape
    for i in range(tiles):
        rows = pl.ds(i * tile, tile)
        total = own[i] + right[rows, :].astype(F32) + left[rows, :].astype(F32)
        out[rows, :] = total.T.astype(BF16)


def quarters_kernel(own, y, core, both, out):
    row = lax.axis_index("row")
    me = lax.rem(row, 2) * 2 + row // 2
    rows = own.shape[0]
    for i, part in enumerate((own, y, core, both)):
        high = lax.rem(me // 2 + i // 2, 2)
        low = lax.rem(me + i % 2, 2)
        out[pl.ds(pl.multiple_of((high * 2 + low) * rows, rows), rows), :] = part[...]


def per_device(n_col, features, tile_values, tile_cols, tile_counts, weight, bias, cotangent):
    node_dev, width = features.shape
    row_tiles, slots, tile, _ = tile_values.shape
    per_dev = node_dev // tile
    col_tiles = n_col * per_dev
    half = n_col // 2
    node_total = node_dev * lax.axis_size("row") * n_col
    grad_scale = 1.0 / math.sqrt(node_total)
    values = tile_values.reshape(row_tiles * slots, tile, tile)

    order = ring_order(n_col)
    right = [(order[i], order[(i + 1) % n_col]) for i in range(n_col)]
    left = [(b, a) for a, b in right]
    cores = [(0, 1), (1, 0), (2, 3), (3, 2)]
    across = [(0, 2), (2, 0), (1, 3), (3, 1)]
    corners = [(0, 3), (3, 0), (1, 2), (2, 1)]
    row = lax.axis_index("row")
    my_y, my_core = row // 2, row % 2

    n_buckets = half + 1
    rank = np.zeros(n_col, np.int64)
    rank[order] = np.arange(n_col)
    place = np.zeros((n_col, col_tiles), np.int32)
    for d in range(n_col):
        for t in range(col_tiles):
            ahead = (rank[t // per_dev] - rank[d]) % n_col
            bucket = min(ahead, n_col - ahead)
            side = 1 if 0 < ahead < half else 0
            place[d, t] = bucket * 256 + side * per_dev + t % per_dev
    tiles = np.arange(row_tiles)
    block = tiles // (row_tiles // 4)
    pos = [
        ((block % 2 != r % 2) * 2 + (block // 2 != r // 2)) * (row_tiles // 4) + tiles % (row_tiles // 4)
        for r in range(4)
    ]
    tables = np.concatenate([np.concatenate(pos), place.reshape(-1)]).astype(np.int32)
    cap = row_tiles * slots + UNIT
    lists = pl.pallas_call(
        functools.partial(lists_kernel, n_buckets, cap, col_tiles, 4 * row_tiles),
        in_specs=[SMEM] * 3,
        out_specs=SMEM,
        out_shape=jax.ShapeDtypeStruct((n_buckets * cap + n_buckets,), jnp.int32),
        compiler_params=params(8),
        cost_estimate=cost(0, 2**12),
        name="lists",
    )(tile_cols, tile_counts.reshape(-1), jnp.asarray(tables))

    dots = 2 * tile * tile * width
    small = cost(dots, tile * tile * 2)
    stream_scratch = [pltpu.VMEM((DEPTH * UNIT, tile, tile), BF16), pltpu.SemaphoreType.DMA((DEPTH * UNIT,))]
    total_shape = jax.ShapeDtypeStruct((row_tiles + 1, tile, width), F32)
    half_shape = jax.ShapeDtypeStruct((row_tiles // 2, tile, width), BF16)

    def forward(bucket, blocks, before, last=False):
        n_tiles = sum(b.shape[0] for b in blocks)
        out = pl.pallas_call(
            functools.partial(forward_kernel, [bucket], cap, n_buckets, len(blocks), len(before), last),
            in_specs=[SMEM, HBM] + [ANY if bucket else HBM] * len(blocks) + [VMEM] * len(before),
            out_specs=[VMEM] * (2 if last else 1),
            out_shape=[half_shape] * 2 if last else [total_shape],
            scratch_shapes=([pltpu.VMEM(total_shape.shape, F32)] if last else [])
            + stream_scratch
            + [pltpu.SemaphoreType.DMA((len(blocks),)), pltpu.VMEM((n_tiles, tile, width), BF16)],
            compiler_params=params(40),
            cost_estimate=small,
            name=f"forward_{bucket}",
        )(lists, values, *blocks, *before)
        return out if last else out[0]

    mine = features.reshape(per_dev, tile, width)
    from_left = from_right = mine
    total = None
    cot_other = None
    for s in range(1, half):
        now = [from_left, from_right] if s > 1 else [mine]
        from_left = lax.ppermute(from_left, "col", right)
        from_right = lax.ppermute(from_right, "col", left)
        if s == 1:
            cot_other = lax.ppermute(cotangent, "row", across)
            from_left, from_right, cot_other, lists = lax.optimization_barrier(
                (from_left, from_right, cot_other, lists)
            )
        else:
            if s == 2:
                total = forward(0, [mine], [])
            total = forward(s - 1, now, [total])
            from_left, from_right, total = lax.optimization_barrier((from_left, from_right, total))
    far_near = lax.ppermute(from_left[: per_dev // 2], "col", right)
    far_away = lax.ppermute(from_right[per_dev // 2 :], "col", left)
    total = forward(half - 1, [from_left, from_right], [total])
    hid_mine, hid_other = forward(half, [far_near, far_away], [total], last=True)

    hid_came = lax.ppermute(hid_other, "row", cores)
    own = (hid_mine.astype(F32) + hid_came.astype(F32)).astype(BF16)
    mid = row_tiles // 4
    own, own_away = own[:mid], own[mid:]
    came = lax.ppermute(own_away, "row", across)
    came_away = lax.ppermute(own, "row", across)

    w_rows = width // 4 + 16
    grad_shape = jax.ShapeDtypeStruct((mid, width, tile), BF16)
    dense_cost = cost(3 * 2 * node_dev * width * width // 4, node_dev * width)
    bias_row = bias.reshape(1, -1)
    layer_out, grad_1, wgrad = pl.pallas_call(
        functools.partial(dense_kernel, False),
        in_specs=[VMEM] * 5,
        out_specs=[VMEM] * 3,
        out_shape=[
            jax.ShapeDtypeStruct((node_dev, width), BF16),
            grad_shape,
            jax.ShapeDtypeStruct((width + 8, width), F32),
        ],
        compiler_params=params(24),
        cost_estimate=dense_cost,
        name="dense_own",
    )(own, came, weight, bias_row, cotangent)
    grad_3 = lax.ppermute(grad_1, "row", cores)
    came_away, layer_out, grad_1, grad_3, wgrad = lax.optimization_barrier(
        (came_away, layer_out, grad_1, grad_3, wgrad)
    )
    grad_2, wgrad = pl.pallas_call(
        functools.partial(dense_kernel, True),
        in_specs=[VMEM] * 6,
        out_specs=[VMEM] * 2,
        out_shape=[grad_shape, jax.ShapeDtypeStruct((4, w_rows, width), F32)],
        compiler_params=params(24),
        cost_estimate=dense_cost,
        name="dense_away",
    )(own_away, came_away, weight, bias_row, cot_other, wgrad)
    grad_4 = lax.ppermute(grad_2, "row", cores)

    wgrad = wgrad.reshape(2, 2, w_rows, width)

    def quarter(core):
        return lax.dynamic_slice(wgrad, (core, my_y, 0, 0), (1, 1, w_rows, width))[0, 0]

    w_sum = quarter(my_core) + lax.ppermute(quarter(1 - my_core), "row", cores)

    def backward(bucket, n_tiles, after=()):
        its_lists, *_ = lax.optimization_barrier((lists, *after))
        return pl.pallas_call(
            functools.partial(backward_kernel, bucket, cap, n_buckets),
            in_specs=[SMEM, HBM] + [ANY] * 4,
            out_specs=VMEM,
            out_shape=jax.ShapeDtypeStruct((n_tiles, width, tile), F32),
            scratch_shapes=[pltpu.VMEM((row_tiles + 1, width, tile), BF16)]
            + stream_scratch
            + [pltpu.SemaphoreType.DMA((4,))],
            compiler_params=params(40),
            cost_estimate=small,
            name=f"backward_{bucket}",
        )(its_lists, values, grad_1, grad_2, grad_3, grad_4)

    def add(local, came):
        return (local + came.astype(F32)).astype(BF16)

    far_part = backward(half, per_dev).astype(BF16)
    cut = per_dev // 2
    sent = lax.optimization_barrier((far_part[:cut], far_part[cut:]))
    stages = [1 << i for i in range((n_col - 1).bit_length())]
    for d in range(half - 1, -1, -1):
        to_right = lax.ppermute(sent[0], "col", right)
        to_left = lax.ppermute(sent[1], "col", left)
        step = half - 1 - d
        quarters = ()
        if step < len(stages):
            w_now, *_ = lax.optimization_barrier((w_sum.astype(BF16), *sent))
            w_came = lax.ppermute(w_now, "col", [(i, i ^ stages[step]) for i in range(n_col)])
            w_sum = w_now.astype(F32) + w_came.astype(F32)
        elif step == len(stages):
            w_now, *_ = lax.optimization_barrier((w_sum * grad_scale, *sent))
            w_own = w_now[: width // 4]
            quarters = [w_own] + [lax.ppermute(w_own, "row", perm) for perm in (across, cores, corners)]
            weight_grad = pl.pallas_call(
                quarters_kernel,
                in_specs=[VMEM] * 4,
                out_specs=VMEM,
                out_shape=jax.ShapeDtypeStruct((width, width), F32),
                compiler_params=params(8),
                cost_estimate=cost(0, 2**12),
                name="quarters",
            )(*quarters)
            bias_grad = w_now[width // 4]
            w_sum = (weight_grad, bias_grad)
        part = backward(d, 2 * per_dev if d else per_dev, sent)
        part, to_right, to_left, w_sum = lax.optimization_barrier((part, to_right, to_left, w_sum))
        if d == 0:
            break
        for_left, for_right = part[:per_dev], part[per_dev:]
        if step == 0:
            sent = (
                jnp.concatenate([add(for_right[:cut], to_right), for_right[cut:].astype(BF16)]),
                jnp.concatenate([for_left[:cut].astype(BF16), add(for_left[cut:], to_left)]),
            )
        else:
            sent = (add(for_right, to_right), add(for_left, to_left))
        sent = lax.optimization_barrier(sent)
    weight_grad, bias_grad = w_sum
    feature_grad = pl.pallas_call(
        finish_kernel,
        in_specs=[VMEM] * 3,
        out_specs=VMEM,
        out_shape=jax.ShapeDtypeStruct((node_dev, width), BF16),
        compiler_params=params(8),
        name="finish",
    )(part, to_right.reshape(node_dev, width), to_left.reshape(node_dev, width))
    return (layer_out, feature_grad, weight_grad, bias_grad)


def solution(mesh):
    placed = (
        P(("row", "col"), None),
        P("col", "row", None, None),
        P("col", "row"),
        P("col", "row"),
        P(),
        P(),
        P(("col", "row"), None),
    )
    return jax.shard_map(
        functools.partial(per_device, mesh.shape["col"]),
        mesh=mesh,
        in_specs=placed,
        out_specs=(P(("col", "row"), None), P(("row", "col"), None), P(), P()),
        check_vma=False,
    )
```

```python
import functools
import math

import jax
import jax.numpy as jnp
import numpy as np
from jax import lax
from jax.experimental import pallas as pl
from jax.experimental.pallas import tpu as pltpu
from jax.sharding import PartitionSpec as P

BF16 = jnp.bfloat16
F32 = jnp.float32
UNIT = 8
DEPTH = 5
AHEAD = 2

VMEM = pl.BlockSpec(memory_space=pltpu.VMEM)
SMEM = pl.BlockSpec(memory_space=pltpu.SMEM)
HBM = pl.BlockSpec(memory_space=pltpu.HBM)
ANY = pl.BlockSpec(memory_space=pl.ANY)


def ring_order(count):
    return list(range(0, count, 2)) + list(range(count - 1, 0, -2))


def params(mib):
    return pltpu.CompilerParams(vmem_limit_bytes=mib * 2**20)


def cost(flops, nbytes):
    return pl.CostEstimate(flops=int(flops), bytes_accessed=int(nbytes), transcendentals=0)


def lists_kernel(n_buckets, cap, col_tiles, place_base, cols, counts, tables, block, lists, kept):
    kept[...] = block[...]
    row_tiles, slots = cols.shape
    ends = n_buckets * cap
    first_place = place_base + lax.axis_index("col") * col_tiles
    first_pos = lax.axis_index("row") * row_tiles
    for b in range(n_buckets):
        lists[ends + b] = 0

    def tile_row(t, _):
        head = t * slots * 65536 + tables[first_pos + t] * 256

        def slot(s, _):
            place = tables[first_place + cols[t, s]]
            bucket = place // 256
            n = lists[ends + bucket]
            lists[bucket * cap + n] = head + s * 65536 + lax.rem(place, 256)
            lists[ends + bucket] = n + 1
            return 0

        lax.fori_loop(0, counts[t], slot, 0)
        return 0

    lax.fori_loop(0, row_tiles, tile_row, 0)
    for b in range(n_buckets):
        n = lists[ends + b]
        units = (n + UNIT - 1) // UNIT

        def fill(i, _, b=b):
            lists[b * cap + i] = row_tiles * 256
            return 0

        lax.fori_loop(n, units * UNIT, fill, 0)
        lists[ends + b] = units


def unit_copies(lists, first, at, values, buffer, sems):
    for u in range(UNIT):
        yield pltpu.make_async_copy(values.at[lists[first + u] // 65536], buffer.at[at + u], sems.at[at + u])


def stream(lists, buckets, cap, n_buckets, values, buffer, sems, between, use, skip=0):
    ends = []
    for b in buckets:
        n = lists[n_buckets * cap + b]
        ends.append(n + (ends[-1] if ends else 0))
    total = ends[-1]

    def locate(g):
        first = buckets[0] * cap + g * UNIT
        for i in range(1, len(buckets)):
            first = jnp.where(g >= ends[i - 1], buckets[i] * cap + (g - ends[i - 1]) * UNIT, first)
        return first

    def copies(g):
        return unit_copies(lists, locate(g), lax.rem(g, DEPTH) * UNIT, values, buffer, sems)

    def ahead(g, _):
        for c in copies(g):
            c.start()
        return 0

    lax.fori_loop(skip, jnp.minimum(total, skip + DEPTH - 1), ahead, 0)
    between()

    def step(g, _):
        @pl.when(g + DEPTH - 1 < total)
        def _():
            ahead(g + DEPTH - 1, 0)

        for c in copies(g):
            c.wait()
        use(locate(g), lax.rem(g, DEPTH) * UNIT, buffer)
        return 0

    lax.fori_loop(skip, total, step, 0)


def destination(entry):
    return lax.rem(entry // 256, 256)


def source(entry):
    return lax.rem(entry, 256)


def forward_kernel(buckets, cap, n_buckets, n_blocks, n_before, role, lists, values, *refs):
    blocks, refs = refs[:n_blocks], refs[n_blocks:]
    before, refs = refs[:n_before], refs[n_before:]
    if role == "last":
        early, refs = refs[0], refs[1:]
    (buffer, sems, block_sems, sources), refs = refs[-4:], refs[:-4]
    total = refs[-1]
    offsets = []
    copies = []
    at = 0
    for i, b in enumerate(blocks):
        copies.append(pltpu.make_async_copy(b, sources.at[pl.ds(at, b.shape[0])], block_sems.at[i]))
        offsets.append(at)
        at += b.shape[0]
    far = n_buckets - 1
    far_units = lists[n_buckets * cap + far]

    if role == "next":
        _, early, early_sems, total = refs[0], refs[1], refs[2], refs[0]
        for g in range(AHEAD):

            @pl.when(g < far_units)
            def _(g=g):
                for c in unit_copies(lists, far * cap + g * UNIT, g * UNIT, values, early, early_sems):
                    c.start()

    def between():
        for c in copies:
            c.start()
        if n_before:
            total[...] = before[0][...]
        else:
            total[...] = jnp.zeros(total.shape, F32)
        for c in copies:
            c.wait()

    def use(first, at, tiles):
        shift = jnp.where(first >= buckets[-1] * cap, offsets[len(buckets) - 1], 0)
        parts = []
        for u in range(UNIT):
            k = source(lists[first + u]) + shift
            parts.append(jnp.dot(tiles[at + u], sources[k], preferred_element_type=F32))
        for u in range(UNIT):
            total[destination(lists[first + u])] += parts[u]

    if role == "last":

        def start():
            between()

            def step(g, _):
                use(far * cap + g * UNIT, g * UNIT, early)
                return 0

            lax.fori_loop(0, jnp.minimum(far_units, AHEAD), step, 0)

        stream(lists, buckets, cap, n_buckets, values, buffer, sems, start, use, skip=AHEAD)
        quarter = refs[0].shape[0]
        for i, out in enumerate(refs[:4]):
            out[...] = total[i * quarter : (i + 1) * quarter].astype(BF16)
    else:
        stream(lists, buckets, cap, n_buckets, values, buffer, sems, between, use)

    if role == "next":
        for g in range(AHEAD):

            @pl.when(g < far_units)
            def _(g=g):
                for c in unit_copies(lists, far * cap + g * UNIT, g * UNIT, values, early, early_sems):
                    c.wait()


def dense_kernel(second, near, away, weight, bias, cot, *refs):
    if second:
        before, grad_t, wgrad = refs
    else:
        out, grad_t, wgrad = refs
    tiles, tile, width = near.shape
    w = weight[...]
    hidden = near[...].reshape(tiles * tile, width).astype(F32) + away[...].reshape(tiles * tile, width).astype(F32)
    hidden = hidden.astype(BF16)
    preact = jnp.dot(hidden, w, preferred_element_type=F32) + bias[...]
    sig = 1.0 / (1.0 + jnp.exp(-preact))
    if not second:
        out[...] = (preact * sig).astype(BF16)
    pgrad = (cot[...].astype(F32) * (sig * (1.0 + preact * (1.0 - sig)))).astype(BF16)
    for i in range(tiles):
        grad_t[i] = lax.dot_general(
            w, pgrad[i * tile : (i + 1) * tile], (((1,), (1,)), ((), ())), preferred_element_type=F32
        ).astype(BF16)
    wg = lax.dot_general(hidden, pgrad, (((0,), (0,)), ((), ())), preferred_element_type=F32)
    bg = jnp.sum(pgrad.astype(F32), axis=0, keepdims=True)
    if second:
        wg = wg + before[:width]
        bg = bg + before[width : width + 1]
        rows = width // 4
        for q in range(4):
            wgrad[q, :rows] = wg[q * rows : (q + 1) * rows]
            wgrad[q, rows:] = jnp.broadcast_to(bg, (wgrad.shape[1] - rows, width))
    else:
        wgrad[:width] = wg
        wgrad[width:] = jnp.broadcast_to(bg, (wgrad.shape[0] - width, width))


def backward_kernel(bucket, cap, n_buckets, n_early, lists, values, *refs):
    early, refs = refs[:n_early], refs[n_early:]
    parts, (out, grads, buffer, sems, part_sems) = refs[:-5], refs[-5:]
    copies = []
    at = 0
    for i, g in enumerate(parts):
        copies.append(pltpu.make_async_copy(g, grads.at[pl.ds(at, g.shape[0])], part_sems.at[i]))
        at += g.shape[0]

    def use(first, at, tiles):
        parts = []
        for u in range(UNIT):
            parts.append(jnp.dot(grads[destination(lists[first + u])], tiles[at + u], preferred_element_type=F32))
        for u in range(UNIT):
            out[source(lists[first + u])] += parts[u]

    def between():
        for c in copies:
            c.start()
        grads[at] = jnp.zeros(grads.shape[1:], BF16)
        out[...] = jnp.zeros(out.shape, F32)
        for c in copies:
            c.wait()
        if n_early:

            def step(g, _):
                use(bucket * cap + g * UNIT, g * UNIT, early[0])
                return 0

            lax.fori_loop(0, jnp.minimum(lists[n_buckets * cap + bucket], AHEAD), step, 0)

    skip = AHEAD if n_early else 0
    stream(lists, [bucket], cap, n_buckets, values, buffer, sems, between, use, skip)


def finish_kernel(own, right, left, out):
    tiles, _, tile = own.shape
    for i in range(tiles):
        rows = pl.ds(i * tile, tile)
        total = own[i] + right[rows, :].astype(F32) + left[rows, :].astype(F32)
        out[rows, :] = total.T.astype(BF16)


def quarters_kernel(own, y, core, both, out):
    row = lax.axis_index("row")
    me = lax.rem(row, 2) * 2 + row // 2
    rows = own.shape[0]
    for i, part in enumerate((own, y, core, both)):
        high = lax.rem(me // 2 + i // 2, 2)
        low = lax.rem(me + i % 2, 2)
        out[pl.ds(pl.multiple_of((high * 2 + low) * rows, rows), rows), :] = part[...]


def per_device(n_col, features, tile_values, tile_cols, tile_counts, weight, bias, cotangent):
    node_dev, width = features.shape
    row_tiles, slots, tile, _ = tile_values.shape
    per_dev = node_dev // tile
    col_tiles = n_col * per_dev
    half = n_col // 2
    node_total = node_dev * lax.axis_size("row") * n_col
    grad_scale = 1.0 / math.sqrt(node_total)
    values = tile_values.reshape(row_tiles * slots, tile, tile)

    order = ring_order(n_col)
    right = [(order[i], order[(i + 1) % n_col]) for i in range(n_col)]
    left = [(b, a) for a, b in right]
    cores = [(0, 1), (1, 0), (2, 3), (3, 2)]
    across = [(0, 2), (2, 0), (1, 3), (3, 1)]
    corners = [(0, 3), (3, 0), (1, 2), (2, 1)]
    row = lax.axis_index("row")
    my_y, my_core = row // 2, row % 2

    n_buckets = half + 1
    rank = np.zeros(n_col, np.int64)
    rank[order] = np.arange(n_col)
    place = np.zeros((n_col, col_tiles), np.int32)
    for d in range(n_col):
        for t in range(col_tiles):
            ahead = (rank[t // per_dev] - rank[d]) % n_col
            bucket = min(ahead, n_col - ahead)
            side = 1 if 0 < ahead < half else 0
            place[d, t] = bucket * 256 + side * per_dev + t % per_dev
    tiles = np.arange(row_tiles)
    block = tiles // (row_tiles // 4)
    pos = [
        ((block % 2 != r % 2) * 2 + (block // 2 != r // 2)) * (row_tiles // 4) + tiles % (row_tiles // 4)
        for r in range(4)
    ]
    tables = np.concatenate([np.concatenate(pos), place.reshape(-1)]).astype(np.int32)
    cap = row_tiles * slots + UNIT
    mine = features.reshape(per_dev, tile, width)
    lists, kept = pl.pallas_call(
        functools.partial(lists_kernel, n_buckets, cap, col_tiles, 4 * row_tiles),
        in_specs=[SMEM] * 3 + [VMEM],
        out_specs=[SMEM, VMEM],
        out_shape=[
            jax.ShapeDtypeStruct((n_buckets * cap + n_buckets,), jnp.int32),
            jax.ShapeDtypeStruct((per_dev, tile, width), BF16),
        ],
        compiler_params=params(8),
        cost_estimate=cost(0, 2**12),
        name="lists",
    )(tile_cols, tile_counts.reshape(-1), jnp.asarray(tables), mine)

    dots = 2 * tile * tile * width
    small = cost(dots, tile * tile * 2)
    stream_scratch = [pltpu.VMEM((DEPTH * UNIT, tile, tile), BF16), pltpu.SemaphoreType.DMA((DEPTH * UNIT,))]
    total_shape = jax.ShapeDtypeStruct((row_tiles + 1, tile, width), F32)
    quarter_shape = jax.ShapeDtypeStruct((row_tiles // 4, tile, width), BF16)

    early_shape = jax.ShapeDtypeStruct((AHEAD * UNIT, tile, tile), BF16)

    def forward(buckets, blocks, before, role="", early=()):
        n_tiles = sum(b.shape[0] for b in blocks)
        scratch = stream_scratch + [
            pltpu.SemaphoreType.DMA((len(blocks),)),
            pltpu.VMEM((n_tiles, tile, width), BF16),
        ]
        out_shape = [total_shape]
        if role == "next":
            out_shape = [total_shape, early_shape]
            scratch = [pltpu.SemaphoreType.DMA((AHEAD * UNIT,))] + scratch
        elif role == "last":
            out_shape = [quarter_shape] * 4
            scratch = [pltpu.VMEM(total_shape.shape, F32)] + scratch
        return pl.pallas_call(
            functools.partial(forward_kernel, buckets, cap, n_buckets, len(blocks), len(before), role),
            in_specs=[SMEM, HBM] + [ANY] * len(blocks) + [VMEM] * (len(before) + len(early)),
            out_specs=[VMEM] * len(out_shape),
            out_shape=out_shape,
            scratch_shapes=scratch,
            compiler_params=params(40),
            cost_estimate=small,
            name=f"forward_{buckets[-1]}",
        )(lists, values, *blocks, *before, *early)

    from_left = from_right = mine
    cot_other = None
    for s in range(1, half):
        now = [from_left, from_right]
        from_left = lax.ppermute(from_left, "col", right)
        from_right = lax.ppermute(from_right, "col", left)
        if s == 1:
            cot_other = lax.ppermute(cotangent, "row", across)
            from_left, from_right, cot_other, lists, kept = lax.optimization_barrier(
                (from_left, from_right, cot_other, lists, kept)
            )
        else:
            if s == 2:
                (total,) = forward([0, 1], [kept, *now], [])
            else:
                (total,) = forward([s - 1], now, [total])
            from_left, from_right, total = lax.optimization_barrier((from_left, from_right, total))
    far_near = lax.ppermute(from_left[: per_dev // 2], "col", right)
    far_away = lax.ppermute(from_right[per_dev // 2 :], "col", left)
    total, early = forward([half - 1], [from_left, from_right], [total], "next")
    own_1, own_2, other_1, other_2 = forward([half], [far_near, far_away], [total], "last", [early])

    def add(local, came):
        return (local.astype(F32) + came.astype(F32)).astype(BF16)

    mid = row_tiles // 4
    came_2 = lax.ppermute(other_2, "row", cores)
    came_1 = lax.ppermute(other_1, "row", cores)
    own_away = add(own_2, came_2)
    came = lax.ppermute(own_away, "row", across)
    own = add(own_1, came_1)
    came_away = lax.ppermute(own, "row", across)

    w_rows = width // 4 + 16
    grad_shape = jax.ShapeDtypeStruct((mid, width, tile), BF16)
    dense_cost = cost(3 * 2 * node_dev * width * width // 4, node_dev * width)
    bias_row = bias.reshape(1, -1)
    layer_out, grad_1, wgrad = pl.pallas_call(
        functools.partial(dense_kernel, False),
        in_specs=[VMEM] * 5,
        out_specs=[VMEM] * 3,
        out_shape=[
            jax.ShapeDtypeStruct((node_dev, width), BF16),
            grad_shape,
            jax.ShapeDtypeStruct((width + 8, width), F32),
        ],
        compiler_params=params(24),
        cost_estimate=dense_cost,
        name="dense_own",
    )(own, came, weight, bias_row, cotangent)
    grad_3 = lax.ppermute(grad_1, "row", cores)
    came_away, layer_out, grad_1, grad_3, wgrad = lax.optimization_barrier(
        (came_away, layer_out, grad_1, grad_3, wgrad)
    )
    grad_2, wgrad = pl.pallas_call(
        functools.partial(dense_kernel, True),
        in_specs=[VMEM] * 6,
        out_specs=[VMEM] * 2,
        out_shape=[grad_shape, jax.ShapeDtypeStruct((4, w_rows, width), F32)],
        compiler_params=params(24),
        cost_estimate=dense_cost,
        name="dense_away",
    )(own_away, came_away, weight, bias_row, cot_other, wgrad)
    grad_4 = lax.ppermute(grad_2, "row", cores)

    wgrad = wgrad.reshape(2, 2, w_rows, width)

    def quarter(core):
        return lax.dynamic_slice(wgrad, (core, my_y, 0, 0), (1, 1, w_rows, width))[0, 0]

    w_sum = quarter(my_core) + lax.ppermute(quarter(1 - my_core), "row", cores)

    def backward(bucket, n_tiles, after=(), early=()):
        its_lists, *_ = lax.optimization_barrier((lists, *after))
        return pl.pallas_call(
            functools.partial(backward_kernel, bucket, cap, n_buckets, len(early)),
            in_specs=[SMEM, HBM] + [VMEM] * len(early) + [ANY] * 4,
            out_specs=VMEM,
            out_shape=jax.ShapeDtypeStruct((n_tiles, width, tile), F32),
            scratch_shapes=[pltpu.VMEM((row_tiles + 1, width, tile), BF16)]
            + stream_scratch
            + [pltpu.SemaphoreType.DMA((4,))],
            compiler_params=params(40),
            cost_estimate=small,
            name=f"backward_{bucket}",
        )(its_lists, values, *early, grad_1, grad_2, grad_3, grad_4)

    far_part = backward(half, per_dev, early=[early]).astype(BF16)
    cut = per_dev // 2
    sent = lax.optimization_barrier((far_part[:cut], far_part[cut:]))
    stages = [1 << i for i in range((n_col - 1).bit_length())]
    for d in range(half - 1, -1, -1):
        to_right = lax.ppermute(sent[0], "col", right)
        to_left = lax.ppermute(sent[1], "col", left)
        step = half - 1 - d
        if step == len(stages):
            w_now, *_ = lax.optimization_barrier((w_sum * grad_scale, *sent))
            w_own = w_now[: width // 4]
            quarters = [w_own] + [lax.ppermute(w_own, "row", perm) for perm in (across, cores, corners)]
            weight_grad = pl.pallas_call(
                quarters_kernel,
                in_specs=[VMEM] * 4,
                out_specs=VMEM,
                out_shape=jax.ShapeDtypeStruct((width, width), F32),
                compiler_params=params(8),
                cost_estimate=cost(0, 2**12),
                name="quarters",
            )(*quarters)
            bias_grad = w_now[width // 4]
        part = backward(d, 2 * per_dev if d else per_dev, sent)
        if step < len(stages):
            w_now, part, *_ = lax.optimization_barrier((w_sum.astype(BF16), part, *sent))
            w_came = lax.ppermute(w_now, "col", [(i, i ^ stages[step]) for i in range(n_col)])
            w_sum = w_now.astype(F32) + w_came.astype(F32)
        if d == 0:
            break
        part, to_right, to_left = lax.optimization_barrier((part, to_right, to_left))
        for_left, for_right = part[:per_dev], part[per_dev:]
        if step == 0:
            sent = (
                jnp.concatenate([add(for_right[:cut], to_right), for_right[cut:].astype(BF16)]),
                jnp.concatenate([for_left[:cut].astype(BF16), add(for_left[cut:], to_left)]),
            )
        else:
            sent = (add(for_right, to_right), add(for_left, to_left))
        sent = lax.optimization_barrier(sent)
    part, to_right, to_left, weight_grad, bias_grad = lax.optimization_barrier(
        (part, to_right, to_left, weight_grad, bias_grad)
    )
    feature_grad = pl.pallas_call(
        finish_kernel,
        in_specs=[VMEM] * 3,
        out_specs=VMEM,
        out_shape=jax.ShapeDtypeStruct((node_dev, width), BF16),
        compiler_params=params(8),
        name="finish",
    )(part, to_right.reshape(node_dev, width), to_left.reshape(node_dev, width))
    return (layer_out, feature_grad, weight_grad, bias_grad)


def solution(mesh):
    placed = (
        P(("row", "col"), None),
        P("col", "row", None, None),
        P("col", "row"),
        P("col", "row"),
        P(),
        P(),
        P(("col", "row"), None),
    )
    return jax.shard_map(
        functools.partial(per_device, mesh.shape["col"]),
        mesh=mesh,
        in_specs=placed,
        out_specs=(P(("col", "row"), None), P(("row", "col"), None), P(), P()),
        check_vma=False,
    )
```

```python
import functools
import math

import jax
import jax.numpy as jnp
import numpy as np
from jax import lax
from jax.experimental import pallas as pl
from jax.experimental.pallas import tpu as pltpu
from jax.sharding import PartitionSpec as P

BF16 = jnp.bfloat16
F32 = jnp.float32
UNIT = 8
DEPTH = 5
AHEAD = 2

VMEM = pl.BlockSpec(memory_space=pltpu.VMEM)
SMEM = pl.BlockSpec(memory_space=pltpu.SMEM)
HBM = pl.BlockSpec(memory_space=pltpu.HBM)
ANY = pl.BlockSpec(memory_space=pl.ANY)


def ring_order(count):
    return list(range(0, count, 2)) + list(range(count - 1, 0, -2))


def params(mib):
    return pltpu.CompilerParams(vmem_limit_bytes=mib * 2**20)


def cost(flops, nbytes):
    return pl.CostEstimate(flops=int(flops), bytes_accessed=int(nbytes), transcendentals=0)


def lists_kernel(n_buckets, cap, col_tiles, place_base, cols, counts, tables, block, lists, kept):
    kept[...] = block[...]
    row_tiles, slots = cols.shape
    ends = n_buckets * cap
    first_place = place_base + lax.axis_index("col") * col_tiles
    first_pos = lax.axis_index("row") * row_tiles
    for b in range(n_buckets):
        lists[ends + b] = 0

    def tile_row(t, _):
        head = t * slots * 65536 + tables[first_pos + t] * 256

        def slot(s, _):
            place = tables[first_place + cols[t, s]]
            bucket = place // 256
            n = lists[ends + bucket]
            lists[bucket * cap + n] = head + s * 65536 + lax.rem(place, 256)
            lists[ends + bucket] = n + 1
            return 0

        lax.fori_loop(0, counts[t], slot, 0)
        return 0

    lax.fori_loop(0, row_tiles, tile_row, 0)
    for b in range(n_buckets):
        n = lists[ends + b]
        units = (n + UNIT - 1) // UNIT

        def fill(i, _, b=b):
            lists[b * cap + i] = row_tiles * 256
            return 0

        lax.fori_loop(n, units * UNIT, fill, 0)
        lists[ends + b] = units


def unit_copies(lists, first, at, values, buffer, sems):
    for u in range(UNIT):
        yield pltpu.make_async_copy(values.at[lists[first + u] // 65536], buffer.at[at + u], sems.at[at + u])


def stream(lists, buckets, cap, n_buckets, values, buffer, sems, between, use, skip=0):
    ends = []
    for b in buckets:
        n = lists[n_buckets * cap + b]
        ends.append(n + (ends[-1] if ends else 0))
    total = ends[-1]

    def locate(g):
        first = buckets[0] * cap + g * UNIT
        for i in range(1, len(buckets)):
            first = jnp.where(g >= ends[i - 1], buckets[i] * cap + (g - ends[i - 1]) * UNIT, first)
        return first

    def copies(g):
        return unit_copies(lists, locate(g), lax.rem(g, DEPTH) * UNIT, values, buffer, sems)

    def ahead(g, _):
        for c in copies(g):
            c.start()
        return 0

    lax.fori_loop(skip, jnp.minimum(total, skip + DEPTH - 1), ahead, 0)
    between()

    def step(g, _):
        @pl.when(g + DEPTH - 1 < total)
        def _():
            ahead(g + DEPTH - 1, 0)

        for c in copies(g):
            c.wait()
        use(locate(g), lax.rem(g, DEPTH) * UNIT, buffer)
        return 0

    lax.fori_loop(skip, total, step, 0)


def destination(entry):
    return lax.rem(entry // 256, 256)


def source(entry):
    return lax.rem(entry, 256)


def forward_kernel(buckets, cap, n_buckets, n_blocks, n_before, role, lists, values, *refs):
    blocks, refs = refs[:n_blocks], refs[n_blocks:]
    before, refs = refs[:n_before], refs[n_before:]
    if role == "last":
        early, refs = refs[0], refs[1:]
    (buffer, sems, block_sems, sources), refs = refs[-4:], refs[:-4]
    total = refs[-1]
    offsets = []
    copies = []
    at = 0
    for i, b in enumerate(blocks):
        copies.append(pltpu.make_async_copy(b, sources.at[pl.ds(at, b.shape[0])], block_sems.at[i]))
        offsets.append(at)
        at += b.shape[0]
    far = n_buckets - 1
    far_units = lists[n_buckets * cap + far]

    if role == "next":
        _, early, early_sems, total = refs[0], refs[1], refs[2], refs[0]
        for g in range(AHEAD):

            @pl.when(g < far_units)
            def _(g=g):
                for c in unit_copies(lists, far * cap + g * UNIT, g * UNIT, values, early, early_sems):
                    c.start()

    def between():
        for c in copies:
            c.start()
        if n_before:
            total[...] = before[0][...]
        else:
            total[...] = jnp.zeros(total.shape, F32)
        for c in copies:
            c.wait()

    def use(first, at, tiles):
        shift = jnp.where(first >= buckets[-1] * cap, offsets[len(buckets) - 1], 0)
        parts = []
        for u in range(UNIT):
            k = source(lists[first + u]) + shift
            parts.append(jnp.dot(tiles[at + u], sources[k], preferred_element_type=F32))
        for u in range(UNIT):
            total[destination(lists[first + u])] += parts[u]

    if role == "last":

        def start():
            between()

            def step(g, _):
                use(far * cap + g * UNIT, g * UNIT, early)
                return 0

            lax.fori_loop(0, jnp.minimum(far_units, AHEAD), step, 0)

        stream(lists, buckets, cap, n_buckets, values, buffer, sems, start, use, skip=AHEAD)
        quarter = refs[0].shape[0]
        for i, out in enumerate(refs[:4]):
            out[...] = total[i * quarter : (i + 1) * quarter].astype(BF16)
    else:
        stream(lists, buckets, cap, n_buckets, values, buffer, sems, between, use)

    if role == "next":
        for g in range(AHEAD):

            @pl.when(g < far_units)
            def _(g=g):
                for c in unit_copies(lists, far * cap + g * UNIT, g * UNIT, values, early, early_sems):
                    c.wait()


def dense_kernel(second, near, away, weight, bias, cot, *refs):
    if second:
        before, grad_t, wgrad = refs
    else:
        out, grad_t, wgrad = refs
    tiles, tile, width = near.shape
    w = weight[...]
    hidden = near[...].reshape(tiles * tile, width).astype(F32) + away[...].reshape(tiles * tile, width).astype(F32)
    hidden = hidden.astype(BF16)
    preact = jnp.dot(hidden, w, preferred_element_type=F32) + bias[...]
    sig = 1.0 / (1.0 + jnp.exp(-preact))
    if not second:
        out[...] = (preact * sig).astype(BF16)
    pgrad = (cot[...].astype(F32) * (sig * (1.0 + preact * (1.0 - sig)))).astype(BF16)
    for i in range(tiles):
        grad_t[i] = lax.dot_general(
            w, pgrad[i * tile : (i + 1) * tile], (((1,), (1,)), ((), ())), preferred_element_type=F32
        ).astype(BF16)
    wg = lax.dot_general(hidden, pgrad, (((0,), (0,)), ((), ())), preferred_element_type=F32)
    bg = jnp.sum(pgrad.astype(F32), axis=0, keepdims=True)
    if second:
        wg = wg + before[:width]
        bg = bg + before[width : width + 1]
        rows = width // 4
        for q in range(4):
            wgrad[q, :rows] = wg[q * rows : (q + 1) * rows]
            wgrad[q, rows:] = jnp.broadcast_to(bg, (wgrad.shape[1] - rows, width))
    else:
        wgrad[:width] = wg
        wgrad[width:] = jnp.broadcast_to(bg, (wgrad.shape[0] - width, width))


def backward_kernel(buckets, shift, sides, cap, n_buckets, n_early, lists, values, *refs):
    swap = lax.rem(lax.axis_index("row"), 2) * sides
    early, refs = refs[:n_early], refs[n_early:]
    parts, (out, grads, buffer, sems, part_sems) = refs[:-5], refs[-5:]
    copies = []
    at = 0
    for i, g in enumerate(parts):
        copies.append(pltpu.make_async_copy(g, grads.at[pl.ds(at, g.shape[0])], part_sems.at[i]))
        at += g.shape[0]

    def use(first, at, tiles):
        parts = []
        for u in range(UNIT):
            parts.append(jnp.dot(grads[destination(lists[first + u])], tiles[at + u], preferred_element_type=F32))
        begin = jnp.where(first // cap == buckets[-1], shift, 0)
        for u in range(UNIT):
            k = source(lists[first + u])
            if sides:
                k = jnp.where(begin == 0, lax.rem(k + swap, 2 * sides), k)
            out[k + begin] += parts[u]

    def between():
        for c in copies:
            c.start()
        grads[at] = jnp.zeros(grads.shape[1:], BF16)
        out[...] = jnp.zeros(out.shape, F32)
        for c in copies:
            c.wait()
        if n_early:

            def step(g, _):
                use(buckets[0] * cap + g * UNIT, g * UNIT, early[0])
                return 0

            lax.fori_loop(0, jnp.minimum(lists[n_buckets * cap + buckets[0]], AHEAD), step, 0)

    skip = AHEAD if n_early else 0
    stream(lists, buckets, cap, n_buckets, values, buffer, sems, between, use, skip)


def finish_kernel(own, right, left, out):
    tiles, _, tile = own.shape
    for i in range(tiles):
        rows = pl.ds(i * tile, tile)
        total = own[i] + right[rows, :].astype(F32) + left[rows, :].astype(F32)
        out[rows, :] = total.T.astype(BF16)


def quarters_kernel(own, y, core, both, out):
    row = lax.axis_index("row")
    me = lax.rem(row, 2) * 2 + row // 2
    rows = own.shape[0]
    for i, part in enumerate((own, y, core, both)):
        high = lax.rem(me // 2 + i // 2, 2)
        low = lax.rem(me + i % 2, 2)
        out[pl.ds(pl.multiple_of((high * 2 + low) * rows, rows), rows), :] = part[...]


def per_device(n_col, features, tile_values, tile_cols, tile_counts, weight, bias, cotangent):
    node_dev, width = features.shape
    row_tiles, slots, tile, _ = tile_values.shape
    per_dev = node_dev // tile
    col_tiles = n_col * per_dev
    half = n_col // 2
    node_total = node_dev * lax.axis_size("row") * n_col
    grad_scale = 1.0 / math.sqrt(node_total)
    values = tile_values.reshape(row_tiles * slots, tile, tile)

    order = ring_order(n_col)
    right = [(order[i], order[(i + 1) % n_col]) for i in range(n_col)]
    left = [(b, a) for a, b in right]
    cores = [(0, 1), (1, 0), (2, 3), (3, 2)]
    across = [(0, 2), (2, 0), (1, 3), (3, 1)]
    corners = [(0, 3), (3, 0), (1, 2), (2, 1)]
    row = lax.axis_index("row")
    my_y, my_core = row // 2, row % 2

    n_buckets = half + 1
    rank = np.zeros(n_col, np.int64)
    rank[order] = np.arange(n_col)
    place = np.zeros((n_col, col_tiles), np.int32)
    for d in range(n_col):
        for t in range(col_tiles):
            ahead = (rank[t // per_dev] - rank[d]) % n_col
            bucket = min(ahead, n_col - ahead)
            side = 1 if 0 < ahead < half else 0
            place[d, t] = bucket * 256 + side * per_dev + t % per_dev
    tiles = np.arange(row_tiles)
    block = tiles // (row_tiles // 4)
    pos = [
        ((block % 2 != r % 2) * 2 + (block // 2 != r // 2)) * (row_tiles // 4) + tiles % (row_tiles // 4)
        for r in range(4)
    ]
    tables = np.concatenate([np.concatenate(pos), place.reshape(-1)]).astype(np.int32)
    cap = row_tiles * slots + UNIT
    mine = features.reshape(per_dev, tile, width)
    lists, kept = pl.pallas_call(
        functools.partial(lists_kernel, n_buckets, cap, col_tiles, 4 * row_tiles),
        in_specs=[SMEM] * 3 + [VMEM],
        out_specs=[SMEM, VMEM],
        out_shape=[
            jax.ShapeDtypeStruct((n_buckets * cap + n_buckets,), jnp.int32),
            jax.ShapeDtypeStruct((per_dev, tile, width), BF16),
        ],
        compiler_params=params(8),
        cost_estimate=cost(0, 2**12),
        name="lists",
    )(tile_cols, tile_counts.reshape(-1), jnp.asarray(tables), mine)

    dots = 2 * tile * tile * width
    small = cost(dots, tile * tile * 2)
    stream_scratch = [pltpu.VMEM((DEPTH * UNIT, tile, tile), BF16), pltpu.SemaphoreType.DMA((DEPTH * UNIT,))]
    total_shape = jax.ShapeDtypeStruct((row_tiles + 1, tile, width), F32)
    quarter_shape = jax.ShapeDtypeStruct((row_tiles // 4, tile, width), BF16)

    early_shape = jax.ShapeDtypeStruct((AHEAD * UNIT, tile, tile), BF16)

    def forward(buckets, blocks, before, role="", early=()):
        n_tiles = sum(b.shape[0] for b in blocks)
        scratch = stream_scratch + [
            pltpu.SemaphoreType.DMA((len(blocks),)),
            pltpu.VMEM((n_tiles, tile, width), BF16),
        ]
        out_shape = [total_shape]
        if role == "next":
            out_shape = [total_shape, early_shape]
            scratch = [pltpu.SemaphoreType.DMA((AHEAD * UNIT,))] + scratch
        elif role == "last":
            out_shape = [quarter_shape] * 4
            scratch = [pltpu.VMEM(total_shape.shape, F32)] + scratch
        return pl.pallas_call(
            functools.partial(forward_kernel, buckets, cap, n_buckets, len(blocks), len(before), role),
            in_specs=[SMEM, HBM] + [ANY] * len(blocks) + [VMEM] * (len(before) + len(early)),
            out_specs=[VMEM] * len(out_shape),
            out_shape=out_shape,
            scratch_shapes=scratch,
            compiler_params=params(40),
            cost_estimate=small,
            name=f"forward_{buckets[-1]}",
        )(lists, values, *blocks, *before, *early)

    from_left = from_right = mine
    cot_other = None
    for s in range(1, half):
        now = [from_left, from_right]
        from_left = lax.ppermute(from_left, "col", right)
        from_right = lax.ppermute(from_right, "col", left)
        if s == 1:
            cot_other = lax.ppermute(cotangent, "row", across)
            from_left, lists, kept = lax.optimization_barrier((from_left, lists, kept))
        else:
            if s == 2:
                (total,) = forward([0, 1], [kept, *now], [])
            else:
                (total,) = forward([s - 1], now, [total])
            if s == 2:
                from_left, total, cot_other = lax.optimization_barrier((from_left, total, cot_other))
            else:
                from_left, total = lax.optimization_barrier((from_left, total))
    far_near = lax.ppermute(from_left[: per_dev // 2], "col", right)
    far_away = lax.ppermute(from_right[per_dev // 2 :], "col", left)
    total, early = forward([half - 1], [from_left, from_right], [total], "next")
    own_1, own_2, other_1, other_2 = forward([half], [far_near, far_away], [total], "last", [early])

    def add(local, came):
        return (local.astype(F32) + came.astype(F32)).astype(BF16)

    mid = row_tiles // 4
    came_2 = lax.ppermute(other_2, "row", cores)
    came_1 = lax.ppermute(other_1, "row", cores)
    own_away = add(own_2, came_2)
    came = lax.ppermute(own_away, "row", across)
    own = add(own_1, came_1)
    came_away = lax.ppermute(own, "row", across)

    w_rows = width // 4 + 16
    grad_shape = jax.ShapeDtypeStruct((mid, width, tile), BF16)
    dense_cost = cost(3 * 2 * node_dev * width * width // 4, node_dev * width)
    bias_row = bias.reshape(1, -1)
    layer_out, grad_1, wgrad = pl.pallas_call(
        functools.partial(dense_kernel, False),
        in_specs=[VMEM] * 5,
        out_specs=[VMEM] * 3,
        out_shape=[
            jax.ShapeDtypeStruct((node_dev, width), BF16),
            grad_shape,
            jax.ShapeDtypeStruct((width + 8, width), F32),
        ],
        compiler_params=params(24),
        cost_estimate=dense_cost,
        name="dense_own",
    )(own, came, weight, bias_row, cotangent)
    grad_3 = lax.ppermute(grad_1, "row", cores)
    came_away, layer_out, grad_1, grad_3, wgrad = lax.optimization_barrier(
        (came_away, layer_out, grad_1, grad_3, wgrad)
    )
    grad_2, wgrad = pl.pallas_call(
        functools.partial(dense_kernel, True),
        in_specs=[VMEM] * 6,
        out_specs=[VMEM] * 2,
        out_shape=[grad_shape, jax.ShapeDtypeStruct((4, w_rows, width), F32)],
        compiler_params=params(24),
        cost_estimate=dense_cost,
        name="dense_away",
    )(own_away, came_away, weight, bias_row, cot_other, wgrad)
    grad_4 = lax.ppermute(grad_2, "row", cores)

    wgrad = wgrad.reshape(2, 2, w_rows, width)

    def quarter(core):
        return lax.dynamic_slice(wgrad, (core, my_y, 0, 0), (1, 1, w_rows, width))[0, 0]

    w_sum = quarter(my_core) + lax.ppermute(quarter(1 - my_core), "row", cores)

    def backward(buckets, n_tiles, after=(), early=()):
        its_lists, *_ = lax.optimization_barrier((lists, *after))
        return pl.pallas_call(
            functools.partial(
                backward_kernel,
                buckets,
                n_tiles - per_dev if len(buckets) > 1 else 0,
                0 if early else per_dev,
                cap,
                n_buckets,
                len(early),
            ),
            in_specs=[SMEM, HBM] + [VMEM] * len(early) + [ANY] * 4,
            out_specs=VMEM,
            out_shape=jax.ShapeDtypeStruct((n_tiles, width, tile), F32),
            scratch_shapes=[pltpu.VMEM((row_tiles + 1, width, tile), BF16)]
            + stream_scratch
            + [pltpu.SemaphoreType.DMA((4,))],
            compiler_params=params(40),
            cost_estimate=small,
            name=f"backward_{buckets[0]}",
        )(its_lists, values, *early, grad_1, grad_2, grad_3, grad_4)

    far_part = backward([half], per_dev, early=[early]).astype(BF16)
    cut = per_dev // 2
    axes = ("row", "col")
    first = [(r * n_col + a, r * n_col + b) for r in range(4) for a, b in (left if r % 2 else right)]
    second = [(b, a) for a, b in first]
    sent = lax.optimization_barrier((far_part[:cut], far_part[cut:]))
    stages = [1 << i for i in range((n_col - 1).bit_length())]
    for d in range(half - 1, -1, -1):
        to_right = lax.ppermute(sent[0], axes, first)
        to_left = lax.ppermute(sent[1], axes, second)
        step = half - 1 - d
        if step == len(stages):
            w_now, *_ = lax.optimization_barrier((w_sum * grad_scale, *sent))
            w_own = w_now[: width // 4]
            quarters = [w_own] + [lax.ppermute(w_own, "row", perm) for perm in (across, cores, corners)]
            weight_grad = pl.pallas_call(
                quarters_kernel,
                in_specs=[VMEM] * 4,
                out_specs=VMEM,
                out_shape=jax.ShapeDtypeStruct((width, width), F32),
                compiler_params=params(8),
                cost_estimate=cost(0, 2**12),
                name="quarters",
            )(*quarters)
            bias_grad = w_now[width // 4]
        if step == 0:
            part = backward([d, 0], 3 * per_dev, sent)
            part, own_part = part[: 2 * per_dev], part[2 * per_dev :]
        elif d:
            part = backward([d], 2 * per_dev, sent)
        if step < len(stages):
            w_now, part, *_ = lax.optimization_barrier((w_sum.astype(BF16), part, *sent))
            w_came = lax.ppermute(w_now, "col", [(i, i ^ stages[step]) for i in range(n_col)])
            w_sum = w_now.astype(F32) + w_came.astype(F32)
        if d == 0:
            break
        part, to_right, to_left = lax.optimization_barrier((part, to_right, to_left))
        for_left, for_right = part[:per_dev], part[per_dev:]
        if step == 0:
            sent = (
                jnp.concatenate([add(for_right[:cut], to_right), for_right[cut:].astype(BF16)]),
                jnp.concatenate([for_left[:cut].astype(BF16), add(for_left[cut:], to_left)]),
            )
        else:
            sent = (add(for_right, to_right), add(for_left, to_left))
    to_right, to_left, weight_grad, bias_grad = lax.optimization_barrier(
        (to_right, to_left, weight_grad, bias_grad)
    )
    feature_grad = pl.pallas_call(
        finish_kernel,
        in_specs=[VMEM] * 3,
        out_specs=VMEM,
        out_shape=jax.ShapeDtypeStruct((node_dev, width), BF16),
        compiler_params=params(8),
        name="finish",
    )(own_part, to_right.reshape(node_dev, width), to_left.reshape(node_dev, width))
    return (layer_out, feature_grad, weight_grad, bias_grad)


def solution(mesh):
    placed = (
        P(("row", "col"), None),
        P("col", "row", None, None),
        P("col", "row"),
        P("col", "row"),
        P(),
        P(),
        P(("col", "row"), None),
    )
    return jax.shard_map(
        functools.partial(per_device, mesh.shape["col"]),
        mesh=mesh,
        in_specs=placed,
        out_specs=(P(("col", "row"), None), P(("row", "col"), None), P(), P()),
        check_vma=False,
    )
```

```python
import functools
import math

import jax
import jax.numpy as jnp
import numpy as np
from jax import lax
from jax.experimental import pallas as pl
from jax.experimental.pallas import tpu as pltpu
from jax.sharding import PartitionSpec as P

BF16 = jnp.bfloat16
F32 = jnp.float32
UNIT = 8
DEPTH = 5
AHEAD = 2

VMEM = pl.BlockSpec(memory_space=pltpu.VMEM)
SMEM = pl.BlockSpec(memory_space=pltpu.SMEM)
HBM = pl.BlockSpec(memory_space=pltpu.HBM)
ANY = pl.BlockSpec(memory_space=pl.ANY)


def ring_order(count):
    return list(range(0, count, 2)) + list(range(count - 1, 0, -2))


def params(mib):
    return pltpu.CompilerParams(vmem_limit_bytes=mib * 2**20)


def cost(flops, nbytes):
    return pl.CostEstimate(flops=int(flops), bytes_accessed=int(nbytes), transcendentals=0)


def lists_kernel(n_buckets, cap, col_tiles, place_base, cols, counts, tables, block, lists, kept):
    kept[...] = block[...]
    row_tiles, slots = cols.shape
    ends = n_buckets * cap
    first_place = place_base + lax.axis_index("col") * col_tiles
    first_pos = lax.axis_index("row") * row_tiles
    for b in range(n_buckets):
        lists[ends + b] = 0

    def tile_row(t, _):
        head = t * slots * 65536 + tables[first_pos + t] * 256

        def slot(s, _):
            place = tables[first_place + cols[t, s]]
            bucket = place // 256
            n = lists[ends + bucket]
            lists[bucket * cap + n] = head + s * 65536 + lax.rem(place, 256)
            lists[ends + bucket] = n + 1
            return 0

        lax.fori_loop(0, counts[t], slot, 0)
        return 0

    lax.fori_loop(0, row_tiles, tile_row, 0)
    for b in range(n_buckets):
        n = lists[ends + b]
        units = (n + UNIT - 1) // UNIT

        def fill(i, _, b=b):
            lists[b * cap + i] = row_tiles * 256
            return 0

        lax.fori_loop(n, units * UNIT, fill, 0)
        lists[ends + b] = units


def unit_copies(lists, first, at, values, buffer, sems):
    for u in range(UNIT):
        yield pltpu.make_async_copy(values.at[lists[first + u] // 65536], buffer.at[at + u], sems.at[at + u])


def stream(lists, buckets, cap, n_buckets, values, buffer, sems, between, use, skip=0):
    ends = []
    for b in buckets:
        n = lists[n_buckets * cap + b]
        ends.append(n + (ends[-1] if ends else 0))
    total = ends[-1]

    def locate(g):
        first = buckets[0] * cap + g * UNIT
        for i in range(1, len(buckets)):
            first = jnp.where(g >= ends[i - 1], buckets[i] * cap + (g - ends[i - 1]) * UNIT, first)
        return first

    def copies(g):
        return unit_copies(lists, locate(g), lax.rem(g, DEPTH) * UNIT, values, buffer, sems)

    def ahead(g, _):
        for c in copies(g):
            c.start()
        return 0

    lax.fori_loop(skip, jnp.minimum(total, skip + DEPTH - 1), ahead, 0)
    between()

    def step(g, _):
        @pl.when(g + DEPTH - 1 < total)
        def _():
            ahead(g + DEPTH - 1, 0)

        for c in copies(g):
            c.wait()
        use(locate(g), lax.rem(g, DEPTH) * UNIT, buffer)
        return 0

    lax.fori_loop(skip, total, step, 0)


def destination(entry):
    return lax.rem(entry // 256, 256)


def source(entry):
    return lax.rem(entry, 256)


def forward_kernel(buckets, cap, n_buckets, n_blocks, n_before, role, lists, values, *refs):
    blocks, refs = refs[:n_blocks], refs[n_blocks:]
    before, refs = refs[:n_before], refs[n_before:]
    if role == "last":
        early, refs = refs[0], refs[1:]
    (buffer, sems, block_sems, sources), refs = refs[-4:], refs[:-4]
    total = refs[-1]
    offsets = []
    copies = []
    at = 0
    for i, b in enumerate(blocks):
        copies.append(pltpu.make_async_copy(b, sources.at[pl.ds(at, b.shape[0])], block_sems.at[i]))
        offsets.append(at)
        at += b.shape[0]
    far = n_buckets - 1
    far_units = lists[n_buckets * cap + far]

    if role == "next":
        _, early, early_sems, total = refs[0], refs[1], refs[2], refs[0]
        for g in range(AHEAD):

            @pl.when(g < far_units)
            def _(g=g):
                for c in unit_copies(lists, far * cap + g * UNIT, g * UNIT, values, early, early_sems):
                    c.start()

    def between():
        for c in copies:
            c.start()
        if n_before:
            total[...] = before[0][...]
        else:
            total[...] = jnp.zeros(total.shape, F32)
        for c in copies:
            c.wait()

    def use(first, at, tiles):
        shift = jnp.where(first >= buckets[-1] * cap, offsets[len(buckets) - 1], 0)
        parts = []
        for u in range(UNIT):
            k = source(lists[first + u]) + shift
            parts.append(jnp.dot(tiles[at + u], sources[k], preferred_element_type=F32))
        for u in range(UNIT):
            total[destination(lists[first + u])] += parts[u]

    if role == "last":

        def start():
            between()

            def step(g, _):
                use(far * cap + g * UNIT, g * UNIT, early)
                return 0

            lax.fori_loop(0, jnp.minimum(far_units, AHEAD), step, 0)

        stream(lists, buckets, cap, n_buckets, values, buffer, sems, start, use, skip=AHEAD)
        quarter = refs[0].shape[0]
        for i, out in enumerate(refs[:4]):
            out[...] = total[i * quarter : (i + 1) * quarter].astype(BF16)
    else:
        stream(lists, buckets, cap, n_buckets, values, buffer, sems, between, use)

    if role == "next":
        for g in range(AHEAD):

            @pl.when(g < far_units)
            def _(g=g):
                for c in unit_copies(lists, far * cap + g * UNIT, g * UNIT, values, early, early_sems):
                    c.wait()


def dense_kernel(second, near, away, weight, bias, cot, *refs):
    if second:
        before, grad_t, wgrad = refs
    else:
        out, grad_t, wgrad = refs
    tiles, tile, width = near.shape
    w = weight[...]
    hidden = near[...].reshape(tiles * tile, width).astype(F32) + away[...].reshape(tiles * tile, width).astype(F32)
    hidden = hidden.astype(BF16)
    preact = jnp.dot(hidden, w, preferred_element_type=F32) + bias[...]
    sig = 1.0 / (1.0 + jnp.exp(-preact))
    if not second:
        out[...] = (preact * sig).astype(BF16)
    pgrad = (cot[...].astype(F32) * (sig * (1.0 + preact * (1.0 - sig)))).astype(BF16)
    for i in range(tiles):
        grad_t[i] = lax.dot_general(
            w, pgrad[i * tile : (i + 1) * tile], (((1,), (1,)), ((), ())), preferred_element_type=F32
        ).astype(BF16)
    wg = lax.dot_general(hidden, pgrad, (((0,), (0,)), ((), ())), preferred_element_type=F32)
    bg = jnp.sum(pgrad.astype(F32), axis=0, keepdims=True)
    if second:
        wg = wg + before[:width]
        bg = bg + before[width : width + 1]
        rows = width // 4
        for q in range(4):
            wgrad[q, :rows] = wg[q * rows : (q + 1) * rows]
            wgrad[q, rows:] = jnp.broadcast_to(bg, (wgrad.shape[1] - rows, width))
    else:
        wgrad[:width] = wg
        wgrad[width:] = jnp.broadcast_to(bg, (wgrad.shape[0] - width, width))


def backward_kernel(buckets, shift, sides, cap, n_buckets, n_early, lists, values, *refs):
    swap = lax.rem(lax.axis_index("row"), 2) * sides
    early, refs = refs[:n_early], refs[n_early:]
    parts, (out, grads, buffer, sems, part_sems) = refs[:-5], refs[-5:]
    copies = []
    at = 0
    for i, g in enumerate(parts):
        copies.append(pltpu.make_async_copy(g, grads.at[pl.ds(at, g.shape[0])], part_sems.at[i]))
        at += g.shape[0]

    def use(first, at, tiles):
        parts = []
        for u in range(UNIT):
            parts.append(jnp.dot(grads[destination(lists[first + u])], tiles[at + u], preferred_element_type=F32))
        begin = jnp.where(first // cap == buckets[-1], shift, 0)
        for u in range(UNIT):
            k = source(lists[first + u])
            if sides:
                k = jnp.where(begin == 0, lax.rem(k + swap, 2 * sides), k)
            out[k + begin] += parts[u]

    def between():
        for c in copies:
            c.start()
        grads[at] = jnp.zeros(grads.shape[1:], BF16)
        out[...] = jnp.zeros(out.shape, F32)
        for c in copies:
            c.wait()
        if n_early:

            def step(g, _):
                use(buckets[0] * cap + g * UNIT, g * UNIT, early[0])
                return 0

            lax.fori_loop(0, jnp.minimum(lists[n_buckets * cap + buckets[0]], AHEAD), step, 0)

    skip = AHEAD if n_early else 0
    stream(lists, buckets, cap, n_buckets, values, buffer, sems, between, use, skip)


def finish_kernel(own, right, left, out):
    tiles, _, tile = own.shape
    for i in range(tiles):
        rows = pl.ds(i * tile, tile)
        total = own[i] + right[rows, :].astype(F32) + left[rows, :].astype(F32)
        out[rows, :] = total.T.astype(BF16)


def quarters_kernel(own, y, core, both, out):
    row = lax.axis_index("row")
    me = lax.rem(row, 2) * 2 + row // 2
    rows = own.shape[0]
    for i, part in enumerate((own, y, core, both)):
        high = lax.rem(me // 2 + i // 2, 2)
        low = lax.rem(me + i % 2, 2)
        out[pl.ds(pl.multiple_of((high * 2 + low) * rows, rows), rows), :] = part[...]


def per_device(n_col, features, tile_values, tile_cols, tile_counts, weight, bias, cotangent):
    node_dev, width = features.shape
    row_tiles, slots, tile, _ = tile_values.shape
    per_dev = node_dev // tile
    col_tiles = n_col * per_dev
    half = n_col // 2
    node_total = node_dev * lax.axis_size("row") * n_col
    grad_scale = 1.0 / math.sqrt(node_total)
    values = tile_values.reshape(row_tiles * slots, tile, tile)

    order = ring_order(n_col)
    right = [(order[i], order[(i + 1) % n_col]) for i in range(n_col)]
    left = [(b, a) for a, b in right]
    cores = [(0, 1), (1, 0), (2, 3), (3, 2)]
    across = [(0, 2), (2, 0), (1, 3), (3, 1)]
    corners = [(0, 3), (3, 0), (1, 2), (2, 1)]
    row = lax.axis_index("row")
    my_y, my_core = row // 2, row % 2

    n_buckets = half + 1
    rank = np.zeros(n_col, np.int64)
    rank[order] = np.arange(n_col)
    place = np.zeros((n_col, col_tiles), np.int32)
    for d in range(n_col):
        for t in range(col_tiles):
            ahead = (rank[t // per_dev] - rank[d]) % n_col
            bucket = min(ahead, n_col - ahead)
            side = 1 if 0 < ahead < half else 0
            place[d, t] = bucket * 256 + side * per_dev + t % per_dev
    tiles = np.arange(row_tiles)
    block = tiles // (row_tiles // 4)
    pos = [
        ((block % 2 != r % 2) * 2 + (block // 2 != r // 2)) * (row_tiles // 4) + tiles % (row_tiles // 4)
        for r in range(4)
    ]
    tables = np.concatenate([np.concatenate(pos), place.reshape(-1)]).astype(np.int32)
    cap = row_tiles * slots + UNIT
    mine = features.reshape(per_dev, tile, width)
    lists, kept = pl.pallas_call(
        functools.partial(lists_kernel, n_buckets, cap, col_tiles, 4 * row_tiles),
        in_specs=[SMEM] * 3 + [VMEM],
        out_specs=[SMEM, VMEM],
        out_shape=[
            jax.ShapeDtypeStruct((n_buckets * cap + n_buckets,), jnp.int32),
            jax.ShapeDtypeStruct((per_dev, tile, width), BF16),
        ],
        compiler_params=params(8),
        cost_estimate=cost(0, 2**12),
        name="lists",
    )(tile_cols, tile_counts.reshape(-1), jnp.asarray(tables), mine)

    dots = 2 * tile * tile * width
    small = cost(dots, tile * tile * 2)
    stream_scratch = [pltpu.VMEM((DEPTH * UNIT, tile, tile), BF16), pltpu.SemaphoreType.DMA((DEPTH * UNIT,))]
    total_shape = jax.ShapeDtypeStruct((row_tiles + 1, tile, width), F32)
    quarter_shape = jax.ShapeDtypeStruct((row_tiles // 4, tile, width), BF16)

    early_shape = jax.ShapeDtypeStruct((AHEAD * UNIT, tile, tile), BF16)

    def forward(buckets, blocks, before, role="", early=()):
        n_tiles = sum(b.shape[0] for b in blocks)
        scratch = stream_scratch + [
            pltpu.SemaphoreType.DMA((len(blocks),)),
            pltpu.VMEM((n_tiles, tile, width), BF16),
        ]
        out_shape = [total_shape]
        if role == "next":
            out_shape = [total_shape, early_shape]
            scratch = [pltpu.SemaphoreType.DMA((AHEAD * UNIT,))] + scratch
        elif role == "last":
            out_shape = [quarter_shape] * 4
            scratch = [pltpu.VMEM(total_shape.shape, F32)] + scratch
        return pl.pallas_call(
            functools.partial(forward_kernel, buckets, cap, n_buckets, len(blocks), len(before), role),
            in_specs=[SMEM, HBM] + [ANY] * len(blocks) + [VMEM] * (len(before) + len(early)),
            out_specs=[VMEM] * len(out_shape),
            out_shape=out_shape,
            scratch_shapes=scratch,
            compiler_params=params(40),
            cost_estimate=small,
            name=f"forward_{buckets[-1]}",
        )(lists, values, *blocks, *before, *early)

    from_left = from_right = mine
    cot_other = None
    for s in range(1, half):
        now = [from_left, from_right]
        from_left = lax.ppermute(from_left, "col", right)
        from_right = lax.ppermute(from_right, "col", left)
        if s == 1:
            cot_other = lax.ppermute(cotangent, "row", across)
            from_left, lists, kept = lax.optimization_barrier((from_left, lists, kept))
        else:
            if s == 2:
                (total,) = forward([0, 1], [kept, *now], [])
            else:
                (total,) = forward([s - 1], now, [total])
            if s == 2:
                from_left, total, cot_other = lax.optimization_barrier((from_left, total, cot_other))
            else:
                from_left, total = lax.optimization_barrier((from_left, total))
    far_near = lax.ppermute(from_left[: per_dev // 2], "col", right)
    far_away = lax.ppermute(from_right[per_dev // 2 :], "col", left)
    total, early = forward([half - 1], [from_left, from_right], [total], "next")
    own_1, own_2, other_1, other_2 = forward([half], [far_near, far_away], [total], "last", [early])

    def add(local, came):
        return (local.astype(F32) + came.astype(F32)).astype(BF16)

    mid = row_tiles // 4
    came_2 = lax.ppermute(other_2, "row", cores)
    came_1 = lax.ppermute(other_1, "row", cores)
    own_away = add(own_2, came_2)
    came = lax.ppermute(own_away, "row", across)
    own = add(own_1, came_1)
    came_away = lax.ppermute(own, "row", across)

    w_rows = width // 4 + 16
    grad_shape = jax.ShapeDtypeStruct((mid, width, tile), BF16)
    dense_cost = cost(3 * 2 * node_dev * width * width // 4, node_dev * width)
    bias_row = bias.reshape(1, -1)
    layer_out, grad_1, wgrad = pl.pallas_call(
        functools.partial(dense_kernel, False),
        in_specs=[VMEM] * 5,
        out_specs=[VMEM] * 3,
        out_shape=[
            jax.ShapeDtypeStruct((node_dev, width), BF16),
            grad_shape,
            jax.ShapeDtypeStruct((width + 8, width), F32),
        ],
        compiler_params=params(24),
        cost_estimate=dense_cost,
        name="dense_own",
    )(own, came, weight, bias_row, cotangent)
    grad_3 = lax.ppermute(grad_1, "row", cores)
    came_away, layer_out, grad_1, grad_3, wgrad = lax.optimization_barrier(
        (came_away, layer_out, grad_1, grad_3, wgrad)
    )
    grad_2, wgrad = pl.pallas_call(
        functools.partial(dense_kernel, True),
        in_specs=[VMEM] * 6,
        out_specs=[VMEM] * 2,
        out_shape=[grad_shape, jax.ShapeDtypeStruct((4, w_rows, width), F32)],
        compiler_params=params(24),
        cost_estimate=dense_cost,
        name="dense_away",
    )(own_away, came_away, weight, bias_row, cot_other, wgrad)
    grad_4 = lax.ppermute(grad_2, "row", cores)

    wgrad = wgrad.reshape(2, 2, w_rows, width)

    def quarter(core):
        return lax.dynamic_slice(wgrad, (core, my_y, 0, 0), (1, 1, w_rows, width))[0, 0]

    w_sum = quarter(my_core) + lax.ppermute(quarter(1 - my_core), "row", cores)

    def backward(buckets, n_tiles, after=(), early=()):
        its_lists, *_ = lax.optimization_barrier((lists, *after))
        return pl.pallas_call(
            functools.partial(
                backward_kernel,
                buckets,
                n_tiles - per_dev if len(buckets) > 1 else 0,
                0 if early else per_dev,
                cap,
                n_buckets,
                len(early),
            ),
            in_specs=[SMEM, HBM] + [VMEM] * len(early) + [ANY] * 4,
            out_specs=VMEM,
            out_shape=jax.ShapeDtypeStruct((n_tiles, width, tile), F32),
            scratch_shapes=[pltpu.VMEM((row_tiles + 1, width, tile), BF16)]
            + stream_scratch
            + [pltpu.SemaphoreType.DMA((4,))],
            compiler_params=params(40),
            cost_estimate=small,
            name=f"backward_{buckets[0]}",
        )(its_lists, values, *early, grad_1, grad_2, grad_3, grad_4)

    far_part = backward([half], per_dev, early=[early]).astype(BF16)
    cut = per_dev // 2
    axes = ("row", "col")
    first = [(r * n_col + a, r * n_col + b) for r in range(4) for a, b in (left if r % 2 else right)]
    second = [(b, a) for a, b in first]
    sent = lax.optimization_barrier((far_part[:cut], far_part[cut:]))
    stages = [1 << i for i in range((n_col - 1).bit_length())]
    for d in range(half - 1, -1, -1):
        to_right = lax.ppermute(sent[0], axes, first)
        to_left = lax.ppermute(sent[1], axes, second)
        step = half - 1 - d
        if step == len(stages):
            w_now, *_ = lax.optimization_barrier((w_sum * grad_scale, *sent))
            w_own = w_now[: width // 4]
            quarters = [w_own] + [lax.ppermute(w_own, "row", perm) for perm in (across, cores, corners)]
            weight_grad = pl.pallas_call(
                quarters_kernel,
                in_specs=[VMEM] * 4,
                out_specs=VMEM,
                out_shape=jax.ShapeDtypeStruct((width, width), F32),
                compiler_params=params(8),
                cost_estimate=cost(0, 2**12),
                name="quarters",
            )(*quarters)
            bias_grad = w_now[width // 4]
        if step == 0:
            part = backward([d, 0], 3 * per_dev, sent)
            part, own_part = part[: 2 * per_dev], part[2 * per_dev :]
        elif d:
            part = backward([d], 2 * per_dev, sent)
        if step < len(stages):
            w_now, *_ = lax.optimization_barrier((w_sum.astype(BF16), *sent))
            w_came = lax.ppermute(w_now, "col", [(i, i ^ stages[step]) for i in range(n_col)])
            w_sum = w_now.astype(F32) + w_came.astype(F32)
        if d == 0:
            break
        part, to_right, to_left = lax.optimization_barrier((part, to_right, to_left))
        for_left, for_right = part[:per_dev], part[per_dev:]
        if step == 0:
            sent = (
                jnp.concatenate([add(for_right[:cut], to_right), for_right[cut:].astype(BF16)]),
                jnp.concatenate([for_left[:cut].astype(BF16), add(for_left[cut:], to_left)]),
            )
        else:
            sent = (add(for_right, to_right), add(for_left, to_left))
    to_right, to_left, weight_grad, bias_grad = lax.optimization_barrier(
        (to_right, to_left, weight_grad, bias_grad)
    )
    feature_grad = pl.pallas_call(
        finish_kernel,
        in_specs=[VMEM] * 3,
        out_specs=VMEM,
        out_shape=jax.ShapeDtypeStruct((node_dev, width), BF16),
        compiler_params=params(8),
        name="finish",
    )(own_part, to_right.reshape(node_dev, width), to_left.reshape(node_dev, width))
    return (layer_out, feature_grad, weight_grad, bias_grad)


def solution(mesh):
    placed = (
        P(("row", "col"), None),
        P("col", "row", None, None),
        P("col", "row"),
        P("col", "row"),
        P(),
        P(),
        P(("col", "row"), None),
    )
    return jax.shard_map(
        functools.partial(per_device, mesh.shape["col"]),
        mesh=mesh,
        in_specs=placed,
        out_specs=(P(("col", "row"), None), P(("row", "col"), None), P(), P()),
        check_vma=False,
    )
```

```python
import functools
import math

import jax
import jax.numpy as jnp
from jax import lax
from jax.experimental import pallas as pl
from jax.experimental.pallas import tpu as pltpu
from jax.sharding import PartitionSpec as P

BF16 = jnp.bfloat16
F32 = jnp.float32
UNIT = 8
DEPTH = 5
AHEAD = 2

VMEM = pl.BlockSpec(memory_space=pltpu.VMEM)
SMEM = pl.BlockSpec(memory_space=pltpu.SMEM)
HBM = pl.BlockSpec(memory_space=pltpu.HBM)
ANY = pl.BlockSpec(memory_space=pl.ANY)


def ring_order(count):
    return list(range(0, count, 2)) + list(range(count - 1, 0, -2))


def params(mib):
    return pltpu.CompilerParams(vmem_limit_bytes=mib * 2**20)


def cost(flops, nbytes):
    return pl.CostEstimate(flops=int(flops), bytes_accessed=int(nbytes), transcendentals=0)


def ring_rank(device, count):
    return jnp.where(lax.rem(device, 2) == 0, device // 2, count - 1 - device // 2)


def lists_kernel(n_buckets, cap, cols, counts, block, lists, kept, places):
    kept[...] = block[...]
    row_tiles, slots = cols.shape
    ends = n_buckets * cap
    row = lax.axis_index("row")
    my_core, my_y = lax.rem(row, 2), row // 2
    half = n_buckets - 1
    n_col = 2 * half
    per_dev = block.shape[0]
    my_rank = ring_rank(lax.axis_index("col"), n_col)

    def find_place(t, _):
        ahead = lax.rem(ring_rank(t // per_dev, n_col) - my_rank + n_col, n_col)
        bucket = jnp.minimum(ahead, n_col - ahead)
        side = ((ahead > 0) & (ahead < half)).astype(jnp.int32)
        places[t] = bucket * 256 + side * per_dev + lax.rem(t, per_dev)
        return 0

    lax.fori_loop(0, places.shape[0], find_place, 0)
    for b in range(n_buckets):
        lists[ends + b] = 0

    def tile_row(t, _):
        owner = t // (row_tiles // 4)
        other_core = (lax.rem(owner, 2) != my_core).astype(jnp.int32)
        other_y = (owner // 2 != my_y).astype(jnp.int32)
        pos = (other_core * 2 + other_y) * (row_tiles // 4) + lax.rem(t, row_tiles // 4)
        head = t * slots * 65536 + pos * 256

        def slot(s, _):
            place = places[cols[t, s]]
            bucket = place >> 8
            n = lists[ends + bucket]
            lists[bucket * cap + n] = head + s * 65536 + (place & 255)
            lists[ends + bucket] = n + 1
            return 0

        lax.fori_loop(0, counts[t], slot, 0)
        return 0

    lax.fori_loop(0, row_tiles, tile_row, 0)
    for b in range(n_buckets):
        n = lists[ends + b]
        units = (n + UNIT - 1) // UNIT

        def fill(i, _, b=b):
            lists[b * cap + i] = row_tiles * 256
            return 0

        lax.fori_loop(n, units * UNIT, fill, 0)
        lists[ends + b] = units


def unit_copies(lists, first, at, values, buffer, sems):
    for u in range(UNIT):
        yield pltpu.make_async_copy(values.at[lists[first + u] >> 16], buffer.at[at + u], sems.at[at + u])


def stream(lists, buckets, cap, n_buckets, values, buffer, sems, between, use, skip=0):
    ends = []
    for b in buckets:
        n = lists[n_buckets * cap + b]
        ends.append(n + (ends[-1] if ends else 0))
    total = ends[-1]

    def locate(g):
        first = buckets[0] * cap + g * UNIT
        for i in range(1, len(buckets)):
            first = jnp.where(g >= ends[i - 1], buckets[i] * cap + (g - ends[i - 1]) * UNIT, first)
        return first

    def copies(g):
        return unit_copies(lists, locate(g), lax.rem(g, DEPTH) * UNIT, values, buffer, sems)

    def ahead(g, _):
        for c in copies(g):
            c.start()
        return 0

    lax.fori_loop(skip, jnp.minimum(total, skip + DEPTH - 1), ahead, 0)
    between()

    def step(g, _):
        @pl.when(g + DEPTH - 1 < total)
        def _():
            ahead(g + DEPTH - 1, 0)

        for c in copies(g):
            c.wait()
        use(locate(g), lax.rem(g, DEPTH) * UNIT, buffer)
        return 0

    lax.fori_loop(skip, total, step, 0)


def destination(entry):
    return (entry >> 8) & 255


def source(entry):
    return entry & 255


def forward_kernel(buckets, cap, n_buckets, n_blocks, n_before, role, lists, values, *refs):
    blocks, refs = refs[:n_blocks], refs[n_blocks:]
    before, refs = refs[:n_before], refs[n_before:]
    if role == "last":
        early, refs = refs[0], refs[1:]
    (buffer, sems, block_sems, sources), refs = refs[-4:], refs[:-4]
    total = refs[-1]
    offsets = []
    copies = []
    at = 0
    for i, b in enumerate(blocks):
        copies.append(pltpu.make_async_copy(b, sources.at[pl.ds(at, b.shape[0])], block_sems.at[i]))
        offsets.append(at)
        at += b.shape[0]
    far = n_buckets - 1
    far_units = lists[n_buckets * cap + far]

    if role == "next":
        _, early, early_sems, total = refs[0], refs[1], refs[2], refs[0]
        for g in range(AHEAD):

            @pl.when(g < far_units)
            def _(g=g):
                for c in unit_copies(lists, far * cap + g * UNIT, g * UNIT, values, early, early_sems):
                    c.start()

    def between():
        for c in copies:
            c.start()
        if n_before:
            total[...] = before[0][...]
        else:
            total[...] = jnp.zeros(total.shape, F32)
        for c in copies:
            c.wait()

    def use(first, at, tiles):
        shift = jnp.where(first >= buckets[-1] * cap, offsets[len(buckets) - 1], 0)
        parts = []
        for u in range(UNIT):
            k = source(lists[first + u]) + shift
            parts.append(jnp.dot(tiles[at + u], sources[k], preferred_element_type=F32))
        for u in range(UNIT):
            total[destination(lists[first + u])] += parts[u]

    if role == "last":

        def start():
            between()

            def step(g, _):
                use(far * cap + g * UNIT, g * UNIT, early)
                return 0

            lax.fori_loop(0, jnp.minimum(far_units, AHEAD), step, 0)

        stream(lists, buckets, cap, n_buckets, values, buffer, sems, start, use, skip=AHEAD)
        quarter = refs[0].shape[0]
        for i, out in enumerate(refs[:4]):
            out[...] = total[i * quarter : (i + 1) * quarter].astype(BF16)
    else:
        stream(lists, buckets, cap, n_buckets, values, buffer, sems, between, use)

    if role == "next":
        for g in range(AHEAD):

            @pl.when(g < far_units)
            def _(g=g):
                for c in unit_copies(lists, far * cap + g * UNIT, g * UNIT, values, early, early_sems):
                    c.wait()


def dense_kernel(second, near, away, weight, bias, cot, *refs):
    if second:
        before, grad_t, wgrad = refs
    else:
        out, grad_t, wgrad = refs
    tiles, tile, width = near.shape
    w = weight[...]
    hidden = near[...].reshape(tiles * tile, width).astype(F32) + away[...].reshape(tiles * tile, width).astype(F32)
    hidden = hidden.astype(BF16)
    preact = jnp.dot(hidden, w, preferred_element_type=F32) + bias[...]
    sig = 1.0 / (1.0 + jnp.exp(-preact))
    if not second:
        out[...] = (preact * sig).astype(BF16)
    pgrad = (cot[...].astype(F32) * (sig * (1.0 + preact * (1.0 - sig)))).astype(BF16)
    for i in range(tiles):
        grad_t[i] = lax.dot_general(
            w, pgrad[i * tile : (i + 1) * tile], (((1,), (1,)), ((), ())), preferred_element_type=F32
        ).astype(BF16)
    wg = lax.dot_general(hidden, pgrad, (((0,), (0,)), ((), ())), preferred_element_type=F32)
    bg = jnp.sum(pgrad.astype(F32), axis=0, keepdims=True)
    if second:
        wg = wg + before[:width]
        bg = bg + before[width : width + 1]
        rows = width // 4
        for q in range(4):
            wgrad[q, :rows] = wg[q * rows : (q + 1) * rows]
            wgrad[q, rows:] = jnp.broadcast_to(bg, (wgrad.shape[1] - rows, width))
    else:
        wgrad[:width] = wg
        wgrad[width:] = jnp.broadcast_to(bg, (wgrad.shape[0] - width, width))


def backward_kernel(buckets, shift, sides, cap, n_buckets, n_early, lists, values, *refs):
    swap = lax.rem(lax.axis_index("row"), 2) * sides
    early, refs = refs[:n_early], refs[n_early:]
    parts, (out, grads, buffer, sems, part_sems) = refs[:-5], refs[-5:]
    copies = []
    at = 0
    for i, g in enumerate(parts):
        copies.append(pltpu.make_async_copy(g, grads.at[pl.ds(at, g.shape[0])], part_sems.at[i]))
        at += g.shape[0]

    def use(first, at, tiles):
        parts = []
        for u in range(UNIT):
            parts.append(jnp.dot(grads[destination(lists[first + u])], tiles[at + u], preferred_element_type=F32))
        begin = jnp.where(first < buckets[0] * cap, shift, 0)
        for u in range(UNIT):
            k = source(lists[first + u])
            if sides:
                moved = jnp.where(k < sides, k + swap, k - swap)
                k = jnp.where(begin == 0, moved, k)
            out[k + begin] += parts[u]

    def between():
        for c in copies:
            c.start()
        grads[at] = jnp.zeros(grads.shape[1:], BF16)
        out[...] = jnp.zeros(out.shape, F32)
        for c in copies:
            c.wait()
        if n_early:

            def step(g, _):
                use(buckets[0] * cap + g * UNIT, g * UNIT, early[0])
                return 0

            lax.fori_loop(0, jnp.minimum(lists[n_buckets * cap + buckets[0]], AHEAD), step, 0)

    skip = AHEAD if n_early else 0
    stream(lists, buckets, cap, n_buckets, values, buffer, sems, between, use, skip)


def finish_kernel(own, right, left, out):
    tiles, _, tile = own.shape
    for i in range(tiles):
        rows = pl.ds(i * tile, tile)
        total = own[i] + right[rows, :].astype(F32) + left[rows, :].astype(F32)
        out[rows, :] = total.T.astype(BF16)


def quarters_kernel(own, y, core, both, out):
    row = lax.axis_index("row")
    me = lax.rem(row, 2) * 2 + row // 2
    rows = own.shape[0]
    for i, part in enumerate((own, y, core, both)):
        high = lax.rem(me // 2 + i // 2, 2)
        low = lax.rem(me + i % 2, 2)
        out[pl.ds(pl.multiple_of((high * 2 + low) * rows, rows), rows), :] = part[...]


def per_device(n_col, features, tile_values, tile_cols, tile_counts, weight, bias, cotangent):
    node_dev, width = features.shape
    row_tiles, slots, tile, _ = tile_values.shape
    per_dev = node_dev // tile
    col_tiles = n_col * per_dev
    half = n_col // 2
    node_total = node_dev * lax.axis_size("row") * n_col
    grad_scale = 1.0 / math.sqrt(node_total)
    values = tile_values.reshape(row_tiles * slots, tile, tile)

    order = ring_order(n_col)
    right = [(order[i], order[(i + 1) % n_col]) for i in range(n_col)]
    left = [(b, a) for a, b in right]
    cores = [(0, 1), (1, 0), (2, 3), (3, 2)]
    across = [(0, 2), (2, 0), (1, 3), (3, 1)]
    corners = [(0, 3), (3, 0), (1, 2), (2, 1)]
    row = lax.axis_index("row")
    my_y, my_core = row // 2, row % 2

    n_buckets = half + 1
    cap = row_tiles * slots + UNIT
    mine = features.reshape(per_dev, tile, width)
    lists, kept = pl.pallas_call(
        functools.partial(lists_kernel, n_buckets, cap),
        in_specs=[SMEM] * 2 + [VMEM],
        out_specs=[SMEM, VMEM],
        out_shape=[
            jax.ShapeDtypeStruct((n_buckets * cap + n_buckets,), jnp.int32),
            jax.ShapeDtypeStruct((per_dev, tile, width), BF16),
        ],
        scratch_shapes=[pltpu.SMEM((col_tiles,), jnp.int32)],
        compiler_params=params(8),
        cost_estimate=cost(0, 2**12),
        name="lists",
    )(tile_cols, tile_counts.reshape(-1), mine)

    dots = 2 * tile * tile * width
    small = cost(dots, tile * tile * 2)
    stream_scratch = [pltpu.VMEM((DEPTH * UNIT, tile, tile), BF16), pltpu.SemaphoreType.DMA((DEPTH * UNIT,))]
    total_shape = jax.ShapeDtypeStruct((row_tiles + 1, tile, width), F32)
    quarter_shape = jax.ShapeDtypeStruct((row_tiles // 4, tile, width), BF16)

    early_shape = jax.ShapeDtypeStruct((AHEAD * UNIT, tile, tile), BF16)

    def forward(buckets, blocks, before, role="", early=()):
        n_tiles = sum(b.shape[0] for b in blocks)
        scratch = stream_scratch + [
            pltpu.SemaphoreType.DMA((len(blocks),)),
            pltpu.VMEM((n_tiles, tile, width), BF16),
        ]
        out_shape = [total_shape]
        if role == "next":
            out_shape = [total_shape, early_shape]
            scratch = [pltpu.SemaphoreType.DMA((AHEAD * UNIT,))] + scratch
        elif role == "last":
            out_shape = [quarter_shape] * 4
            scratch = [pltpu.VMEM(total_shape.shape, F32)] + scratch
        return pl.pallas_call(
            functools.partial(forward_kernel, buckets, cap, n_buckets, len(blocks), len(before), role),
            in_specs=[SMEM, HBM] + [ANY] * len(blocks) + [VMEM] * (len(before) + len(early)),
            out_specs=[VMEM] * len(out_shape),
            out_shape=out_shape,
            scratch_shapes=scratch,
            compiler_params=params(40),
            cost_estimate=small,
            name=f"forward_{buckets[-1]}",
        )(lists, values, *blocks, *before, *early)

    from_left = from_right = mine
    cot_other = None
    for s in range(1, half):
        now = [from_left, from_right]
        from_left = lax.ppermute(from_left, "col", right)
        from_right = lax.ppermute(from_right, "col", left)
        if s == 1:
            cot_other = lax.ppermute(cotangent, "row", across)
            from_left, lists, kept = lax.optimization_barrier((from_left, lists, kept))
        else:
            if s == 2:
                (total,) = forward([0, 1], [kept, *now], [])
            else:
                (total,) = forward([s - 1], now, [total])
            if s == 2:
                from_left, total, cot_other = lax.optimization_barrier((from_left, total, cot_other))
            else:
                from_left, total = lax.optimization_barrier((from_left, total))
    far_near = lax.ppermute(from_left[: per_dev // 2], "col", right)
    far_away = lax.ppermute(from_right[per_dev // 2 :], "col", left)
    total, early = forward([half - 1], [from_left, from_right], [total], "next")
    own_1, own_2, other_1, other_2 = forward([half], [far_near, far_away], [total], "last", [early])

    def add(local, came):
        return (local.astype(F32) + came.astype(F32)).astype(BF16)

    mid = row_tiles // 4
    came_2 = lax.ppermute(other_2, "row", cores)
    came_1 = lax.ppermute(other_1, "row", cores)
    own_away = add(own_2, came_2)
    came = lax.ppermute(own_away, "row", across)
    own = add(own_1, came_1)
    came_away = lax.ppermute(own, "row", across)

    w_rows = width // 4 + 16
    grad_shape = jax.ShapeDtypeStruct((mid, width, tile), BF16)
    dense_cost = cost(3 * 2 * node_dev * width * width // 4, node_dev * width)
    bias_row = bias.reshape(1, -1)
    layer_out, grad_1, wgrad = pl.pallas_call(
        functools.partial(dense_kernel, False),
        in_specs=[VMEM] * 5,
        out_specs=[VMEM] * 3,
        out_shape=[
            jax.ShapeDtypeStruct((node_dev, width), BF16),
            grad_shape,
            jax.ShapeDtypeStruct((width + 8, width), F32),
        ],
        compiler_params=params(24),
        cost_estimate=dense_cost,
        name="dense_own",
    )(own, came, weight, bias_row, cotangent)
    grad_3 = lax.ppermute(grad_1, "row", cores)
    came_away, layer_out, grad_1, grad_3, wgrad = lax.optimization_barrier(
        (came_away, layer_out, grad_1, grad_3, wgrad)
    )
    grad_2, wgrad = pl.pallas_call(
        functools.partial(dense_kernel, True),
        in_specs=[VMEM] * 6,
        out_specs=[VMEM] * 2,
        out_shape=[grad_shape, jax.ShapeDtypeStruct((4, w_rows, width), F32)],
        compiler_params=params(24),
        cost_estimate=dense_cost,
        name="dense_away",
    )(own_away, came_away, weight, bias_row, cot_other, wgrad)
    grad_4 = lax.ppermute(grad_2, "row", cores)

    wgrad = wgrad.reshape(2, 2, w_rows, width)

    def quarter(core):
        return lax.dynamic_slice(wgrad, (core, my_y, 0, 0), (1, 1, w_rows, width))[0, 0]

    w_sum = quarter(my_core) + lax.ppermute(quarter(1 - my_core), "row", cores)

    def backward(buckets, n_tiles, after=(), early=()):
        its_lists, *_ = lax.optimization_barrier((lists, *after))
        return pl.pallas_call(
            functools.partial(
                backward_kernel,
                buckets,
                n_tiles - per_dev if len(buckets) > 1 else 0,
                0 if early else per_dev,
                cap,
                n_buckets,
                len(early),
            ),
            in_specs=[SMEM, HBM] + [VMEM] * len(early) + [ANY] * 4,
            out_specs=VMEM,
            out_shape=jax.ShapeDtypeStruct((n_tiles, width, tile), F32),
            scratch_shapes=[pltpu.VMEM((row_tiles + 1, width, tile), BF16)]
            + stream_scratch
            + [pltpu.SemaphoreType.DMA((4,))],
            compiler_params=params(40),
            cost_estimate=small,
            name=f"backward_{buckets[0]}",
        )(its_lists, values, *early, grad_1, grad_2, grad_3, grad_4)

    far_part = backward([half], per_dev, early=[early]).astype(BF16)
    cut = per_dev // 2
    axes = ("row", "col")
    first = [(r * n_col + a, r * n_col + b) for r in range(4) for a, b in (left if r % 2 else right)]
    second = [(b, a) for a, b in first]
    sent = lax.optimization_barrier((far_part[:cut], far_part[cut:]))
    stages = [1 << i for i in range((n_col - 1).bit_length())]
    for d in range(half - 1, -1, -1):
        to_right = lax.ppermute(sent[0], axes, first)
        to_left = lax.ppermute(sent[1], axes, second)
        step = half - 1 - d
        if step == len(stages):
            w_now, *_ = lax.optimization_barrier((w_sum * grad_scale, *sent))
            w_own = w_now[: width // 4]
            quarters = [w_own] + [lax.ppermute(w_own, "row", perm) for perm in (across, cores, corners)]
            weight_grad = pl.pallas_call(
                quarters_kernel,
                in_specs=[VMEM] * 4,
                out_specs=VMEM,
                out_shape=jax.ShapeDtypeStruct((width, width), F32),
                compiler_params=params(8),
                cost_estimate=cost(0, 2**12),
                name="quarters",
            )(*quarters)
            bias_grad = w_now[width // 4]
        if step == 0:
            part = backward([d, 0], 3 * per_dev, sent)
            part, own_part = part[: 2 * per_dev], part[2 * per_dev :]
        elif d:
            part = backward([d], 2 * per_dev, sent)
        if step < len(stages):
            w_now, *_ = lax.optimization_barrier((w_sum.astype(BF16), *sent))
            w_came = lax.ppermute(w_now, "col", [(i, i ^ stages[step]) for i in range(n_col)])
            w_sum = w_now.astype(F32) + w_came.astype(F32)
        if d == 0:
            break
        part, to_right, to_left = lax.optimization_barrier((part, to_right, to_left))
        for_left, for_right = part[:per_dev], part[per_dev:]
        if step == 0:
            sent = (
                jnp.concatenate([add(for_right[:cut], to_right), for_right[cut:].astype(BF16)]),
                jnp.concatenate([for_left[:cut].astype(BF16), add(for_left[cut:], to_left)]),
            )
        else:
            sent = (add(for_right, to_right), add(for_left, to_left))
    to_right, to_left, weight_grad, bias_grad = lax.optimization_barrier(
        (to_right, to_left, weight_grad, bias_grad)
    )
    feature_grad = pl.pallas_call(
        finish_kernel,
        in_specs=[VMEM] * 3,
        out_specs=VMEM,
        out_shape=jax.ShapeDtypeStruct((node_dev, width), BF16),
        compiler_params=params(8),
        name="finish",
    )(own_part, to_right.reshape(node_dev, width), to_left.reshape(node_dev, width))
    return (layer_out, feature_grad, weight_grad, bias_grad)


def solution(mesh):
    placed = (
        P(("row", "col"), None),
        P("col", "row", None, None),
        P("col", "row"),
        P("col", "row"),
        P(),
        P(),
        P(("col", "row"), None),
    )
    return jax.shard_map(
        functools.partial(per_device, mesh.shape["col"]),
        mesh=mesh,
        in_specs=placed,
        out_specs=(P(("col", "row"), None), P(("row", "col"), None), P(), P()),
        check_vma=False,
    )
```

```python
import functools
import math

import jax
import jax.numpy as jnp
from jax import lax
from jax.experimental import pallas as pl
from jax.experimental.pallas import tpu as pltpu
from jax.sharding import PartitionSpec as P

BF16 = jnp.bfloat16
F32 = jnp.float32
UNIT = 8
DEPTH = 5
AHEAD = 2

VMEM = pl.BlockSpec(memory_space=pltpu.VMEM)
SMEM = pl.BlockSpec(memory_space=pltpu.SMEM)
HBM = pl.BlockSpec(memory_space=pltpu.HBM)
ANY = pl.BlockSpec(memory_space=pl.ANY)


def ring_order(count):
    return list(range(0, count, 2)) + list(range(count - 1, 0, -2))


def params(mib):
    return pltpu.CompilerParams(vmem_limit_bytes=mib * 2**20)


def cost(flops, nbytes):
    return pl.CostEstimate(flops=int(flops), bytes_accessed=int(nbytes), transcendentals=0)


def ring_rank(device, count):
    return jnp.where(lax.rem(device, 2) == 0, device // 2, count - 1 - device // 2)


def lists_kernel(n_buckets, cap, cols, counts, block, lists, kept, places):
    kept[...] = block[...]
    row_tiles, slots = cols.shape
    ends = n_buckets * cap
    row = lax.axis_index("row")
    my_core, my_y = lax.rem(row, 2), row // 2
    half = n_buckets - 1
    n_col = 2 * half
    per_dev = block.shape[0]
    my_rank = ring_rank(lax.axis_index("col"), n_col)

    def find_place(t, _):
        ahead = lax.rem(ring_rank(t // per_dev, n_col) - my_rank + n_col, n_col)
        bucket = jnp.minimum(ahead, n_col - ahead)
        side = ((ahead > 0) & (ahead < half)).astype(jnp.int32)
        places[t] = bucket * 256 + side * per_dev + lax.rem(t, per_dev)
        return 0

    lax.fori_loop(0, places.shape[0], find_place, 0)
    for b in range(n_buckets):
        lists[ends + b] = 0

    def tile_row(t, _):
        owner = t // (row_tiles // 4)
        other_core = (lax.rem(owner, 2) != my_core).astype(jnp.int32)
        other_y = (owner // 2 != my_y).astype(jnp.int32)
        pos = (other_core * 2 + other_y) * (row_tiles // 4) + lax.rem(t, row_tiles // 4)
        head = t * slots * 65536 + pos * 256

        def slot(s, _):
            place = places[cols[t, s]]
            bucket = place >> 8
            n = lists[ends + bucket]
            lists[bucket * cap + n] = head + s * 65536 + (place & 255)
            lists[ends + bucket] = n + 1
            return 0

        lax.fori_loop(0, counts[t], slot, 0)
        return 0

    lax.fori_loop(0, row_tiles, tile_row, 0)
    for b in range(n_buckets):
        n = lists[ends + b]
        units = (n + UNIT - 1) // UNIT

        def fill(i, _, b=b):
            lists[b * cap + i] = row_tiles * 256
            return 0

        lax.fori_loop(n, units * UNIT, fill, 0)
        lists[ends + b] = units


def unit_copies(lists, first, at, values, buffer, sems):
    for u in range(UNIT):
        yield pltpu.make_async_copy(values.at[lists[first + u] >> 16], buffer.at[at + u], sems.at[at + u])


def stream(lists, buckets, cap, n_buckets, values, buffer, sems, between, use, skip=0):
    ends = []
    for b in buckets:
        n = lists[n_buckets * cap + b]
        ends.append(n + (ends[-1] if ends else 0))
    total = ends[-1]

    def locate(g):
        first = buckets[0] * cap + g * UNIT
        for i in range(1, len(buckets)):
            first = jnp.where(g >= ends[i - 1], buckets[i] * cap + (g - ends[i - 1]) * UNIT, first)
        return first

    def copies(g):
        return unit_copies(lists, locate(g), lax.rem(g, DEPTH) * UNIT, values, buffer, sems)

    def ahead(g, _):
        for c in copies(g):
            c.start()
        return 0

    lax.fori_loop(skip, jnp.minimum(total, skip + DEPTH - 1), ahead, 0)
    between()

    def step(g, _):
        @pl.when(g + DEPTH - 1 < total)
        def _():
            ahead(g + DEPTH - 1, 0)

        for c in copies(g):
            c.wait()
        use(locate(g), lax.rem(g, DEPTH) * UNIT, buffer)
        return 0

    lax.fori_loop(skip, total, step, 0)


def destination(entry):
    return (entry >> 8) & 255


def source(entry):
    return entry & 255


def forward_kernel(buckets, cap, n_buckets, n_blocks, n_before, role, lists, values, *refs):
    blocks, refs = refs[:n_blocks], refs[n_blocks:]
    before, refs = refs[:n_before], refs[n_before:]
    if role == "last":
        early, refs = refs[0], refs[1:]
    (buffer, sems, block_sems, sources), refs = refs[-4:], refs[:-4]
    total = refs[-1]
    offsets = []
    copies = []
    at = 0
    for i, b in enumerate(blocks):
        copies.append(pltpu.make_async_copy(b, sources.at[pl.ds(at, b.shape[0])], block_sems.at[i]))
        offsets.append(at)
        at += b.shape[0]
    far = n_buckets - 1
    far_units = lists[n_buckets * cap + far]

    if role == "next":
        _, early, early_sems, total = refs[0], refs[1], refs[2], refs[0]
        for g in range(AHEAD):

            @pl.when(g < far_units)
            def _(g=g):
                for c in unit_copies(lists, far * cap + g * UNIT, g * UNIT, values, early, early_sems):
                    c.start()

    def between():
        for c in copies:
            c.start()
        if n_before:
            total[...] = before[0][...]
        else:
            total[...] = jnp.zeros(total.shape, F32)
        for c in copies:
            c.wait()

    def use(first, at, tiles):
        shift = jnp.where(first >= buckets[-1] * cap, offsets[len(buckets) - 1], 0)
        parts = []
        for u in range(UNIT):
            k = source(lists[first + u]) + shift
            parts.append(jnp.dot(tiles[at + u], sources[k], preferred_element_type=F32))
        for u in range(UNIT):
            total[destination(lists[first + u])] += parts[u]

    if role == "last":

        def start():
            between()

            def step(g, _):
                use(far * cap + g * UNIT, g * UNIT, early)
                return 0

            lax.fori_loop(0, jnp.minimum(far_units, AHEAD), step, 0)

        stream(lists, buckets, cap, n_buckets, values, buffer, sems, start, use, skip=AHEAD)
        quarter = refs[0].shape[0]
        for i, out in enumerate(refs[:4]):
            out[...] = total[i * quarter : (i + 1) * quarter].astype(BF16)
    else:
        stream(lists, buckets, cap, n_buckets, values, buffer, sems, between, use)

    if role == "next":
        for g in range(AHEAD):

            @pl.when(g < far_units)
            def _(g=g):
                for c in unit_copies(lists, far * cap + g * UNIT, g * UNIT, values, early, early_sems):
                    c.wait()


def dense_kernel(second, near, away, weight, bias, cot, *refs):
    if second:
        before, grad_t, wgrad = refs
    else:
        out, grad_t, wgrad = refs
    tiles, tile, width = near.shape
    w = weight[...]
    hidden = near[...].reshape(tiles * tile, width).astype(F32) + away[...].reshape(tiles * tile, width).astype(F32)
    hidden = hidden.astype(BF16)
    preact = jnp.dot(hidden, w, preferred_element_type=F32) + bias[...]
    sig = 1.0 / (1.0 + jnp.exp(-preact))
    if not second:
        out[...] = (preact * sig).astype(BF16)
    pgrad = (cot[...].astype(F32) * (sig * (1.0 + preact * (1.0 - sig)))).astype(BF16)
    for i in range(tiles):
        grad_t[i] = lax.dot_general(
            w, pgrad[i * tile : (i + 1) * tile], (((1,), (1,)), ((), ())), preferred_element_type=F32
        ).astype(BF16)
    wg = lax.dot_general(hidden, pgrad, (((0,), (0,)), ((), ())), preferred_element_type=F32)
    bg = jnp.sum(pgrad.astype(F32), axis=0, keepdims=True)
    if second:
        wg = wg + before[:width]
        bg = bg + before[width : width + 1]
        rows = width // 4
        for q in range(4):
            wgrad[q, :rows] = wg[q * rows : (q + 1) * rows]
            wgrad[q, rows:] = jnp.broadcast_to(bg, (wgrad.shape[1] - rows, width))
    else:
        wgrad[:width] = wg
        wgrad[width:] = jnp.broadcast_to(bg, (wgrad.shape[0] - width, width))


def backward_kernel(buckets, shift, sides, cap, n_buckets, n_early, lists, values, *refs):
    swap = lax.rem(lax.axis_index("row"), 2) * sides
    early, refs = refs[:n_early], refs[n_early:]
    parts, (out, grads, buffer, sems, part_sems) = refs[:-5], refs[-5:]
    copies = []
    at = 0
    for i, g in enumerate(parts):
        copies.append(pltpu.make_async_copy(g, grads.at[pl.ds(at, g.shape[0])], part_sems.at[i]))
        at += g.shape[0]

    def use(first, at, tiles):
        parts = []
        for u in range(UNIT):
            parts.append(jnp.dot(grads[destination(lists[first + u])], tiles[at + u], preferred_element_type=F32))
        begin = jnp.where(first < buckets[0] * cap, shift, 0)
        for u in range(UNIT):
            k = source(lists[first + u])
            if sides:
                moved = jnp.where(k < sides, k + swap, k - swap)
                k = jnp.where(begin == 0, moved, k)
            out[k + begin] += parts[u]

    def between():
        for c in copies:
            c.start()
        grads[at] = jnp.zeros(grads.shape[1:], BF16)
        out[...] = jnp.zeros(out.shape, F32)
        for c in copies:
            c.wait()
        if n_early:

            def step(g, _):
                use(buckets[0] * cap + g * UNIT, g * UNIT, early[0])
                return 0

            lax.fori_loop(0, jnp.minimum(lists[n_buckets * cap + buckets[0]], AHEAD), step, 0)

    skip = AHEAD if n_early else 0
    stream(lists, buckets, cap, n_buckets, values, buffer, sems, between, use, skip)


def finish_kernel(own, right, left, out):
    tiles, _, tile = own.shape
    for i in range(tiles):
        rows = pl.ds(i * tile, tile)
        total = own[i] + right[rows, :].astype(F32) + left[rows, :].astype(F32)
        out[rows, :] = total.T.astype(BF16)


def quarters_kernel(own, y, core, both, out):
    row = lax.axis_index("row")
    me = lax.rem(row, 2) * 2 + row // 2
    rows = own.shape[0]
    for i, part in enumerate((own, y, core, both)):
        high = lax.rem(me // 2 + i // 2, 2)
        low = lax.rem(me + i % 2, 2)
        out[pl.ds(pl.multiple_of((high * 2 + low) * rows, rows), rows), :] = part[...]


def per_device(n_col, features, tile_values, tile_cols, tile_counts, weight, bias, cotangent):
    node_dev, width = features.shape
    row_tiles, slots, tile, _ = tile_values.shape
    per_dev = node_dev // tile
    col_tiles = n_col * per_dev
    half = n_col // 2
    node_total = node_dev * lax.axis_size("row") * n_col
    grad_scale = 1.0 / math.sqrt(node_total)
    values = tile_values.reshape(row_tiles * slots, tile, tile)

    order = ring_order(n_col)
    right = [(order[i], order[(i + 1) % n_col]) for i in range(n_col)]
    left = [(b, a) for a, b in right]
    cores = [(0, 1), (1, 0), (2, 3), (3, 2)]
    across = [(0, 2), (2, 0), (1, 3), (3, 1)]
    corners = [(0, 3), (3, 0), (1, 2), (2, 1)]
    row = lax.axis_index("row")
    my_y, my_core = row // 2, row % 2

    n_buckets = half + 1
    cap = row_tiles * slots + UNIT
    mine = features.reshape(per_dev, tile, width)
    lists, kept = pl.pallas_call(
        functools.partial(lists_kernel, n_buckets, cap),
        in_specs=[SMEM] * 2 + [VMEM],
        out_specs=[SMEM, VMEM],
        out_shape=[
            jax.ShapeDtypeStruct((n_buckets * cap + n_buckets,), jnp.int32),
            jax.ShapeDtypeStruct((per_dev, tile, width), BF16),
        ],
        scratch_shapes=[pltpu.SMEM((col_tiles,), jnp.int32)],
        compiler_params=params(8),
        cost_estimate=cost(0, 2**12),
        name="lists",
    )(tile_cols, tile_counts.reshape(-1), mine)

    dots = 2 * tile * tile * width
    small = cost(dots, tile * tile * 2)
    stream_scratch = [pltpu.VMEM((DEPTH * UNIT, tile, tile), BF16), pltpu.SemaphoreType.DMA((DEPTH * UNIT,))]
    total_shape = jax.ShapeDtypeStruct((row_tiles + 1, tile, width), F32)
    quarter_shape = jax.ShapeDtypeStruct((row_tiles // 4, tile, width), BF16)

    early_shape = jax.ShapeDtypeStruct((AHEAD * UNIT, tile, tile), BF16)

    def forward(buckets, blocks, before, role="", early=()):
        n_tiles = sum(b.shape[0] for b in blocks)
        scratch = stream_scratch + [
            pltpu.SemaphoreType.DMA((len(blocks),)),
            pltpu.VMEM((n_tiles, tile, width), BF16),
        ]
        out_shape = [total_shape]
        if role == "next":
            out_shape = [total_shape, early_shape]
            scratch = [pltpu.SemaphoreType.DMA((AHEAD * UNIT,))] + scratch
        elif role == "last":
            out_shape = [quarter_shape] * 4
            scratch = [pltpu.VMEM(total_shape.shape, F32)] + scratch
        return pl.pallas_call(
            functools.partial(forward_kernel, buckets, cap, n_buckets, len(blocks), len(before), role),
            in_specs=[SMEM, HBM] + [ANY] * len(blocks) + [VMEM] * (len(before) + len(early)),
            out_specs=[VMEM] * len(out_shape),
            out_shape=out_shape,
            scratch_shapes=scratch,
            compiler_params=params(40),
            cost_estimate=small,
            name=f"forward_{buckets[-1]}",
        )(lists, values, *blocks, *before, *early)

    from_left = from_right = mine
    for s in range(1, half):
        now = [from_left, from_right]
        from_left = lax.ppermute(from_left, "col", right)
        from_right = lax.ppermute(from_right, "col", left)
        if s == 1:
            from_left, lists, kept = lax.optimization_barrier((from_left, lists, kept))
        else:
            if s == 2:
                (total,) = forward([0, 1], [kept, *now], [])
            else:
                (total,) = forward([s - 1], now, [total])
            from_left, total = lax.optimization_barrier((from_left, total))
    cot_sent, total = lax.optimization_barrier((cotangent, total))
    cot_other = lax.ppermute(cot_sent, "row", across)
    far_near = lax.ppermute(from_left[: per_dev // 2], "col", right)
    far_away = lax.ppermute(from_right[per_dev // 2 :], "col", left)
    total, early = forward([half - 1], [from_left, from_right], [total], "next")
    far_near, cot_other = lax.optimization_barrier((far_near, cot_other))
    own_1, own_2, other_1, other_2 = forward([half], [far_near, far_away], [total], "last", [early])

    def add(local, came):
        return (local.astype(F32) + came.astype(F32)).astype(BF16)

    mid = row_tiles // 4
    came_2 = lax.ppermute(other_2, "row", cores)
    came_1 = lax.ppermute(other_1, "row", cores)
    own_away = add(own_2, came_2)
    came = lax.ppermute(own_away, "row", across)
    own = add(own_1, came_1)
    came_away = lax.ppermute(own, "row", across)

    w_rows = width // 4 + 16
    grad_shape = jax.ShapeDtypeStruct((mid, width, tile), BF16)
    dense_cost = cost(3 * 2 * node_dev * width * width // 4, node_dev * width)
    bias_row = bias.reshape(1, -1)
    layer_out, grad_1, wgrad = pl.pallas_call(
        functools.partial(dense_kernel, False),
        in_specs=[VMEM] * 5,
        out_specs=[VMEM] * 3,
        out_shape=[
            jax.ShapeDtypeStruct((node_dev, width), BF16),
            grad_shape,
            jax.ShapeDtypeStruct((width + 8, width), F32),
        ],
        compiler_params=params(24),
        cost_estimate=dense_cost,
        name="dense_own",
    )(own, came, weight, bias_row, cotangent)
    grad_3 = lax.ppermute(grad_1, "row", cores)
    came_away, layer_out, grad_1, grad_3, wgrad = lax.optimization_barrier(
        (came_away, layer_out, grad_1, grad_3, wgrad)
    )
    grad_2, wgrad = pl.pallas_call(
        functools.partial(dense_kernel, True),
        in_specs=[VMEM] * 6,
        out_specs=[VMEM] * 2,
        out_shape=[grad_shape, jax.ShapeDtypeStruct((4, w_rows, width), F32)],
        compiler_params=params(24),
        cost_estimate=dense_cost,
        name="dense_away",
    )(own_away, came_away, weight, bias_row, cot_other, wgrad)
    grad_4 = lax.ppermute(grad_2, "row", cores)

    wgrad = wgrad.reshape(2, 2, w_rows, width)

    def quarter(core):
        return lax.dynamic_slice(wgrad, (core, my_y, 0, 0), (1, 1, w_rows, width))[0, 0]

    w_sum = quarter(my_core) + lax.ppermute(quarter(1 - my_core), "row", cores)

    def backward(buckets, n_tiles, after=(), early=()):
        its_lists, *_ = lax.optimization_barrier((lists, *after))
        return pl.pallas_call(
            functools.partial(
                backward_kernel,
                buckets,
                n_tiles - per_dev if len(buckets) > 1 else 0,
                0 if early else per_dev,
                cap,
                n_buckets,
                len(early),
            ),
            in_specs=[SMEM, HBM] + [VMEM] * len(early) + [ANY] * 4,
            out_specs=VMEM,
            out_shape=jax.ShapeDtypeStruct((n_tiles, width, tile), F32),
            scratch_shapes=[pltpu.VMEM((row_tiles + 1, width, tile), BF16)]
            + stream_scratch
            + [pltpu.SemaphoreType.DMA((4,))],
            compiler_params=params(40),
            cost_estimate=small,
            name=f"backward_{buckets[0]}",
        )(its_lists, values, *early, grad_1, grad_2, grad_3, grad_4)

    far_part = backward([half], per_dev, early=[early]).astype(BF16)
    cut = per_dev // 2
    axes = ("row", "col")
    first = [(r * n_col + a, r * n_col + b) for r in range(4) for a, b in (left if r % 2 else right)]
    second = [(b, a) for a, b in first]
    sent = lax.optimization_barrier((far_part[:cut], far_part[cut:]))
    stages = [1 << i for i in range((n_col - 1).bit_length())]
    for d in range(half - 1, -1, -1):
        to_right = lax.ppermute(sent[0], axes, first)
        to_left = lax.ppermute(sent[1], axes, second)
        step = half - 1 - d
        if step == len(stages):
            w_now, *_ = lax.optimization_barrier((w_sum * grad_scale, *sent))
            w_own = w_now[: width // 4]
            quarters = [w_own] + [lax.ppermute(w_own, "row", perm) for perm in (across, cores, corners)]
            weight_grad = pl.pallas_call(
                quarters_kernel,
                in_specs=[VMEM] * 4,
                out_specs=VMEM,
                out_shape=jax.ShapeDtypeStruct((width, width), F32),
                compiler_params=params(8),
                cost_estimate=cost(0, 2**12),
                name="quarters",
            )(*quarters)
            bias_grad = w_now[width // 4]
        if step == 0:
            part = backward([d, 0], 3 * per_dev, sent)
            part, own_part = part[: 2 * per_dev], part[2 * per_dev :]
        elif d:
            part = backward([d], 2 * per_dev, sent)
        if step < len(stages):
            w_now, *_ = lax.optimization_barrier((w_sum.astype(BF16), *sent))
            w_came = lax.ppermute(w_now, "col", [(i, i ^ stages[step]) for i in range(n_col)])
            w_sum = w_now.astype(F32) + w_came.astype(F32)
        if d == 0:
            break
        part, to_right, to_left = lax.optimization_barrier((part, to_right, to_left))
        for_left, for_right = part[:per_dev], part[per_dev:]
        if step == 0:
            sent = (
                jnp.concatenate([add(for_right[:cut], to_right), for_right[cut:].astype(BF16)]),
                jnp.concatenate([for_left[:cut].astype(BF16), add(for_left[cut:], to_left)]),
            )
        else:
            sent = (add(for_right, to_right), add(for_left, to_left))
    to_right, to_left, weight_grad, bias_grad = lax.optimization_barrier(
        (to_right, to_left, weight_grad, bias_grad)
    )
    feature_grad = pl.pallas_call(
        finish_kernel,
        in_specs=[VMEM] * 3,
        out_specs=VMEM,
        out_shape=jax.ShapeDtypeStruct((node_dev, width), BF16),
        compiler_params=params(8),
        name="finish",
    )(own_part, to_right.reshape(node_dev, width), to_left.reshape(node_dev, width))
    return (layer_out, feature_grad, weight_grad, bias_grad)


def solution(mesh):
    placed = (
        P(("row", "col"), None),
        P("col", "row", None, None),
        P("col", "row"),
        P("col", "row"),
        P(),
        P(),
        P(("col", "row"), None),
    )
    return jax.shard_map(
        functools.partial(per_device, mesh.shape["col"]),
        mesh=mesh,
        in_specs=placed,
        out_specs=(P(("col", "row"), None), P(("row", "col"), None), P(), P()),
        check_vma=False,
    )
```
